32 devices in a mesh: dp: 2 (over x), ctx: 4 (over z), mp: 4 (over y, core).
Axes of the slice: x: 2, y: 2, z: 4, core: 2. Of those that a mesh axis runs over, the one named last changes fastest.
Arguments:
- inputs: bfloat16 [1, 1024, 2048], P(None, ('dp', 'ctx'), 'mp'), may hold values from -6 to 6
- doc_start: int32 [1, 1024], P(None, ('dp', 'ctx')), may hold values 0 or 1
- gate_weight: bfloat16 [256, 8, 512], P(None, 'mp'), may hold values from -0.375 to 0.375
- gate_bias: float32 [8, 512], P('mp'), may hold values from -4 to 4
- decay_rate: float32 [2048], P('mp'), may hold values from 1.953125e-05 to 0.08, as said below
- cotangent: bfloat16 [1, 1024, 2048], P(None, ('dp', 'ctx'), 'mp'), may hold values from -0.59765625 to 0.59765625
Outputs:
- outputs: bfloat16 [1, 1024, 2048], P(None, ('dp', 'ctx'), 'mp')
- grad_inputs: bfloat16 [1, 1024, 2048], P(None, ('dp', 'ctx'), 'mp')
- grad_gate_weight: float32 [256, 8, 512], P(('dp', 'ctx'), 'mp')
The draws below stay inside these ranges and needn't reach their ends.
Inputs may be any that keep to these rules, and one draw needn't show every extreme that they name: `decay_rate`: each channel's rate is either slow, between 0.02 / 1024 and 0.2 / 1024, or fast, between 0.02 and 0.08, in any mix.
All inputs are finite; a program needn't handle non-finite values. No bound on the sum of `doc_start` on one device may be relied on, other than what follows from the above.
Results may differ from the reference program's by a relative error of at most 0.0028.
Values sent between devices are 32-bit elements; how exact they have to be, the bound alone decides.
A program may use at most 64 MiB of HBM per device.

```python
import jax
import jax.numpy as jnp
from jax import lax

HEADS = 8
HD = 256
D = 2048
SEQ = 1024
BATCH = 1


def draw_decay_rate(key, part):
    base = jax.random.fold_in(key, 7)
    key_pick, key_slow, key_fast = jax.random.split(base, 3)
    slow_share = 0.5
    picked = jax.random.uniform(key_pick, (D,), jnp.float32)
    slow = jnp.exp(jax.random.uniform(key_slow, (D,), jnp.float32, jnp.log(0.02 / SEQ), jnp.log(0.2 / SEQ)))
    fast = jnp.exp(jax.random.uniform(key_fast, (D,), jnp.float32, jnp.log(0.02), jnp.log(0.08)))
    return jnp.where(picked < slow_share, slow, fast).astype(jnp.float32)


def plant(result, key, low, high):
    place = [jax.random.randint(jax.random.fold_in(key, axis), (), 0, length) for axis, length in enumerate(result.shape)]
    longest = result.shape.index(max(result.shape))
    next_to = place[:longest] + [(place[longest] + 1) % result.shape[longest]] + place[longest + 1:]
    return result.at[tuple(place)].set(low).at[tuple(next_to)].set(high)


def block_scale(key, shape, cuts, smallest, top_value):
    loudness, own = 1.0, jax.random.fold_in(key, 6)
    for dim, blocks in cuts:
        heights = jnp.exp(jax.random.uniform(jax.random.fold_in(own, dim), (blocks,), jnp.float32, smallest / len(cuts), top_value / len(cuts)))
        loudness = loudness * jnp.repeat(heights, shape[dim] // blocks).reshape([-1 if axis == dim else 1 for axis in range(len(shape))])
    return loudness


def gaussian(stream_key, extent, spread, most, cuts=(), dtype=jnp.bfloat16):
    level = block_scale(stream_key, extent, cuts, -0.22, 0.18) if cuts else 1.0
    result = jax.random.normal(stream_key, extent, jnp.float32) * spread * level
    return jnp.minimum(jnp.maximum(result, -most), most).astype(dtype)


def setup_inputs(seed: int = 0) -> dict:
    key_of = jax.random.split(jax.random.key(seed), 7)
    inputs = gaussian(key_of[0], (BATCH, SEQ, D), 1.0, 6.0, ((1, 8), (2, 4)))
    doc_start = plant((jax.random.randint(key_of[1], (BATCH, SEQ), 0, SEQ // 4) < 1).astype(jnp.int32), jax.random.fold_in(key_of[1], 1), 0, 1)
    gate_weight = gaussian(key_of[2], (HD, HEADS, 2 * HD), HD ** -0.5, 0.375, ((1, 4),))
    gate_bias = gaussian(key_of[3], (HEADS, 2 * HD), 1.0, 4.0, ((0, 4),), jnp.float32)
    decay_rate = draw_decay_rate(jax.random.fold_in(key_of[6], 71), 0)
    cotangent = gaussian(key_of[5], (BATCH, SEQ, D), 0.1, 0.59765625, ((1, 8), (2, 4)))
    return {"inputs": inputs, "doc_start": doc_start, "gate_weight": gate_weight, "gate_bias": gate_bias, "decay_rate": decay_rate, "cotangent": cotangent}


def linear_link(first, second):
    return (first[0] * second[0], second[0] * first[1] + second[1])

def head_pass(pieces):
    x_head, w_head, b_head, r_head, g_head, keep = pieces
    width = x_head.shape[2]
    x_float = x_head.astype(jnp.float32)
    pre = jnp.einsum('bsk,km->bsm', x_float, w_head.astype(jnp.float32)) + b_head
    rgate = jax.nn.sigmoid(pre[..., :width])
    igate = jax.nn.sigmoid(pre[..., width:])
    decay = jnp.exp(-8.0 * rgate * r_head)
    keep3 = keep[..., None]
    carry = decay * keep3
    root = jnp.sqrt(1.0 - decay * decay + 0.01)
    scale = jnp.where(keep3 > 0.5, root, jnp.float32(1.0))
    drive = scale * igate * x_float
    cumul, state = lax.associative_scan(linear_link, (carry, drive), axis=1)
    outputs = state.astype(jnp.bfloat16)
    grad_out = g_head.astype(jnp.float32)
    ones_col = jnp.ones_like(carry[:, :1])
    shifted = jnp.concatenate([carry[:, 1:], ones_col], axis=1)
    pcum, adjoint = lax.associative_scan(linear_link, (shifted, grad_out), reverse=True, axis=1)
    previous = jnp.concatenate([jnp.zeros_like(state[:, :1]), state[:, :-1]], axis=1)
    dscale = jnp.where(keep3 > 0.5, -decay * decay / root, jnp.float32(0.0))
    dlog = adjoint * keep3 * decay * previous + adjoint * igate * x_float * dscale
    dgate = dlog * (-8.0 * r_head) * rgate * (1.0 - rgate)
    dinput = adjoint * scale * x_float * igate * (1.0 - igate)
    dpre = jnp.concatenate([dgate, dinput], axis=-1).astype(jnp.bfloat16)
    dpre_float = dpre.astype(jnp.float32)
    grad_x = adjoint * scale * igate + jnp.einsum('bsm,km->bsk', dpre_float, w_head.astype(jnp.float32))
    grad_w = jnp.einsum('bsk,bsm->km', x_float, dpre_float)
    return (outputs, grad_x.astype(jnp.bfloat16), grad_w)

def reference(inputs, doc_start, gate_weight, gate_bias, decay_rate, cotangent):
    batch_rows, seq_len, width_all = inputs.shape
    heads = gate_weight.shape[1]
    head_dim = gate_weight.shape[0]
    keep = 1.0 - doc_start.astype(jnp.float32)
    x_heads = jnp.moveaxis(inputs.reshape(batch_rows, seq_len, heads, head_dim), 2, 0)
    g_heads = jnp.moveaxis(cotangent.reshape(batch_rows, seq_len, heads, head_dim), 2, 0)
    w_heads = jnp.moveaxis(gate_weight, 1, 0)
    r_heads = decay_rate.reshape(heads, head_dim)

    def one_head(items):
        x_head, w_head, b_head, r_head, g_head = items
        return head_pass((x_head, w_head, b_head, r_head, g_head, keep))
    outs, grads, wgrads = lax.map(one_head, (x_heads, w_heads, gate_bias, r_heads, g_heads))
    outputs = jnp.moveaxis(outs, 0, 2).reshape(batch_rows, seq_len, width_all)
    grad_inputs = jnp.moveaxis(grads, 0, 2).reshape(batch_rows, seq_len, width_all)
    grad_gate_weight = jnp.moveaxis(wgrads, 0, 1)
    return (outputs, grad_inputs, grad_gate_weight)
```

```python
import functools

import jax
import jax.numpy as jnp
from jax import lax
from jax.experimental import pallas as pl
from jax.experimental.pallas import tpu as pltpu
from jax.sharding import PartitionSpec as P

MESH = pl.DeviceIdType.MESH
SUB = 8


def kernel(
    dps, ctxs, x_ref, doc_ref, w_ref, bias_ref, rate_ref, g_ref, out_ref, gx_ref, gw_ref,
    xf, xb, xt, gf, pre, carry_s, s_s, p_s, la_s, q_s, c1a_s, c1b_s, c2_s, c3_s, outp, dpre,
    gxp, sums, sums_in, gwp, recv1, sbuf, recv2,
    sum_send, sum_recv, one_send, one_recv, two_send, two_recv,
):
    rows, width = x_ref.shape
    heads, hd, hm = w_ref.shape
    count = dps * ctxs
    steps = rows // SUB
    my_dp, my_ctx = lax.axis_index("dp"), lax.axis_index("ctx")
    me = my_dp * ctxs + my_ctx
    f32, bf16 = jnp.float32, jnp.bfloat16

    barrier = pltpu.get_barrier_semaphore()
    for d in range(1, count):
        to = lax.rem(me + d, count)
        pl.semaphore_signal(
            barrier, inc=1, device_id={"dp": to // ctxs, "ctx": lax.rem(to, ctxs)},
            device_id_type=MESH,
        )

    row = lax.broadcasted_iota(jnp.int32, (rows, rows), 0)
    col = lax.broadcasted_iota(jnp.int32, (rows, rows), 1)
    here = (row % SUB) * steps + row // SUB == col
    back_here = (col % SUB) * steps + col // SUB == row
    perm = jnp.where(here, 1.0, 0.0).astype(bf16)
    unperm = jnp.where(back_here, 1.0, 0.0).astype(bf16)
    keep_col = 1.0 - jnp.sum(
        jnp.where(here, doc_ref[...].astype(f32), 0.0), axis=1, keepdims=True
    )
    xf[...] = jnp.dot(perm, x_ref[...], preferred_element_type=f32)
    xb[...] = xf[...].astype(bf16)
    gf[...] = jnp.dot(perm, g_ref[...], preferred_element_type=f32)
    chunk = lax.broadcasted_iota(jnp.int32, (SUB, hd), 0)

    ends = []
    for h in range(heads):
        ch = slice(h * hd, (h + 1) * hd)
        pre[...] = (
            jnp.dot(xb[:, ch], w_ref[h], preferred_element_type=f32) + bias_ref[h : h + 1, :]
        )
        rate8 = -8.0 * rate_ref[:, ch]
        state = prod = None
        for i in range(steps):
            rs = slice(i * SUB, (i + 1) * SUB)
            x = xf[rs, ch]
            keep = jnp.broadcast_to(keep_col[rs], (SUB, hd))
            kept = keep > 0.5
            rgate = 0.5 * jnp.tanh(0.5 * pre[rs, :hd]) + 0.5
            igate = 0.5 * jnp.tanh(0.5 * pre[rs, hd:]) + 0.5
            decay = jnp.exp(rate8 * rgate)
            square = decay * decay
            inside = 1.0 - square + 0.01
            inverse = lax.rsqrt(inside)
            carry = decay * keep
            scale = jnp.where(kept, inside * inverse, 1.0)
            c3 = scale * igate
            gated = igate * x
            drive = scale * gated
            c1 = rate8 * rgate * (1.0 - rgate)
            carry_s[rs, ch] = carry
            c1a_s[rs, ch] = carry * c1
            c1b_s[rs, ch] = gated * jnp.where(kept, -square * inverse, 0.0) * c1
            c2_s[rs, ch] = drive * (1.0 - igate)
            c3_s[rs, ch] = c3
            if i == 0:
                state, prod = drive, carry
            else:
                state, prod = carry * state + drive, carry * prod
            s_s[rs, ch] = state
            p_s[rs, ch] = prod
        adj = gf[(steps - 1) * SUB :, ch]
        tail = jnp.ones((SUB, hd), f32)
        la_s[(steps - 1) * SUB :, ch] = adj
        q_s[(steps - 1) * SUB :, ch] = tail
        for i in range(steps - 2, -1, -1):
            rs = slice(i * SUB, (i + 1) * SUB)
            after = carry_s[(i + 1) * SUB : (i + 2) * SUB, ch]
            adj = gf[rs, ch] + after * adj
            tail = after * tail
            la_s[rs, ch] = adj
            q_s[rs, ch] = tail
        first = carry_s[:SUB, ch]
        fs, fp = state, prod
        bu, bp = first * adj, prod
        s = 1
        while s < SUB:
            ok = chunk >= s
            rolled_p, rolled_s = pltpu.roll(fp, s, 0), pltpu.roll(fs, s, 0)
            fs = jnp.where(ok, fp * rolled_s + fs, fs)
            fp = jnp.where(ok, fp * rolled_p, fp)
            ok = chunk < SUB - s
            rolled_p, rolled_s = pltpu.roll(bp, SUB - s, 0), pltpu.roll(bu, SUB - s, 0)
            bu = jnp.where(ok, bp * rolled_s + bu, bu)
            bp = jnp.where(ok, bp * rolled_p, bp)
            s *= 2
        for l in range(hd // 128):
            lanes = slice(l * 128, (l + 1) * 128)
            at = h * (hd // 128) + l
            half = width // 128
            sums[0, at : at + 1] = fp[SUB - 1 :, lanes]
            sums[1, at : at + 1] = fp[SUB - 1 :, lanes]
            sums[0, half + at : half + at + 1] = bu[:1, lanes]
            sums[1, half + at : half + at + 1] = fs[SUB - 1 :, lanes]
        ends.append((
            jnp.where(chunk >= 1, pltpu.roll(fp, 1, 0), 1.0),
            jnp.where(chunk >= 1, pltpu.roll(fs, 1, 0), 0.0),
            jnp.where(chunk < SUB - 1, pltpu.roll(bp, SUB - 1, 0), 1.0),
            jnp.where(chunk < SUB - 1, pltpu.roll(bu, SUB - 1, 0), 0.0),
        ))

    pl.semaphore_wait(barrier, count - 1)
    sends = []
    summaries = []
    for d in range(1, count):
        to = lax.rem(me + d, count)
        copy = pltpu.make_async_remote_copy(
            src_ref=sums.at[(to - me + count) // count],
            dst_ref=sums_in.at[d - 1],
            send_sem=sum_send.at[d - 1],
            recv_sem=sum_recv.at[d - 1],
            device_id={"dp": to // ctxs, "ctx": lax.rem(to, ctxs)},
            device_id_type=MESH,
        )
        copy.start()
        sends.append(copy)
        summaries.append(copy)

    for h in range(heads):
        ch = slice(h * hd, (h + 1) * hd)
        xt[ch, :] = jnp.transpose(xf[:, ch]).astype(bf16)

    for copy in summaries:
        copy.wait_recv()
    half = width // 128
    state_in = jnp.zeros((half, 128), f32)
    adj_in = jnp.zeros((half, 128), f32)
    for d in range(count - 1, 0, -1):
        longer = sums_in[d - 1, :half] * state_in + sums_in[d - 1, half:]
        state_in = jnp.where(d <= me, longer, state_in)
        after = count - d - 1
        longer = sums_in[after, :half] * adj_in + sums_in[after, half:]
        adj_in = jnp.where(me + d < count, longer, adj_in)

    def lanes_of(value, h):
        per = hd // 128
        return jnp.concatenate([value[h * per + l : h * per + l + 1] for l in range(per)], axis=1)

    block = ctxs * (hd // count)
    stage_one = {}
    for h in range(heads):
        ch = slice(h * hd, (h + 1) * hd)
        ex_p, ex_s, ex_q, ex_u = ends[h]
        start = ex_s + ex_p * lanes_of(state_in, h)
        prev = start
        enter = ex_u + ex_q * lanes_of(adj_in, h)
        for i in range(0, steps, 2):
            got = []
            for j in (i, i + 1):
                rs = slice(j * SUB, (j + 1) * SUB)
                state = s_s[rs, ch] + p_s[rs, ch] * start
                adj = la_s[rs, ch] + q_s[rs, ch] * enter
                dgate = adj * (c1a_s[rs, ch] * prev + c1b_s[rs, ch])
                got.append((state, dgate, adj * c2_s[rs, ch], adj * c3_s[rs, ch]))
                prev = state
            both = slice(i * SUB, (i + 2) * SUB)
            outp[both, ch] = jnp.concatenate([got[0][0], got[1][0]]).astype(bf16)
            dpre[both, h * hm : h * hm + hd] = jnp.concatenate([got[0][1], got[1][1]]).astype(bf16)
            dpre[both, h * hm + hd : (h + 1) * hm] = jnp.concatenate(
                [got[0][2], got[1][2]]
            ).astype(bf16)
            gxp[both, ch] = jnp.concatenate([got[0][3], got[1][3]])
        for d in list(range(1, dps)) + [0]:
            to_dp = lax.rem(my_dp + d, dps)
            left = xt[pl.ds(pl.multiple_of(h * hd + to_dp * block, block), block), :]
            part = jnp.dot(left, dpre[:, h * hm : (h + 1) * hm], preferred_element_type=f32)
            gwp[h, to_dp] = part.reshape(ctxs, hd // count, hm)
            if d == 0:
                continue
            for c in list(range(1, ctxs)) + [0]:
                to_ctx = lax.rem(my_ctx + c, ctxs)
                copy = pltpu.make_async_remote_copy(
                    src_ref=gwp.at[h, to_dp, to_ctx],
                    dst_ref=recv1.at[h, d - 1, c],
                    send_sem=one_send.at[h, d - 1, c],
                    recv_sem=one_recv.at[h, d - 1, c],
                    device_id={"dp": to_dp},
                    device_id_type=MESH,
                )
                copy.start()
                sends.append(copy)
                stage_one[h, d, c] = copy

    def finish(h):
        ch = slice(h * hd, (h + 1) * hd)
        back = lax.dot_general(
            dpre[:, h * hm : (h + 1) * hm], w_ref[h], (((1,), (1,)), ((), ())),
            preferred_element_type=f32,
        )
        whole = (gxp[:, ch] + back).astype(bf16)
        gx_ref[:, ch] = jnp.dot(unperm, whole, preferred_element_type=f32).astype(bf16)
        out_ref[:, ch] = jnp.dot(unperm, outp[:, ch], preferred_element_type=f32).astype(bf16)

    for h in range(heads):
        finish(h)

    stage_two = {}
    for h in range(heads):
        for c in list(range(1, ctxs)) + [0]:
            to_ctx = lax.rem(my_ctx + c, ctxs)
            total = gwp[h, my_dp, to_ctx]
            for d in range(1, dps):
                stage_one[h, d, c].wait_recv()
                total = total + recv1[h, d - 1, c]
            if c == 0:
                gw_ref[h] = total
                continue
            sbuf[h, c - 1] = total
            copy = pltpu.make_async_remote_copy(
                src_ref=sbuf.at[h, c - 1],
                dst_ref=recv2.at[h, c - 1],
                send_sem=two_send.at[h, c - 1],
                recv_sem=two_recv.at[h, c - 1],
                device_id={"ctx": to_ctx},
                device_id_type=MESH,
            )
            copy.start()
            sends.append(copy)
            stage_two[h, c] = copy
    for h in range(heads):
        total = gw_ref[h]
        for c in range(1, ctxs):
            stage_two[h, c].wait_recv()
            total = total + recv2[h, c - 1]
        gw_ref[h] = total
    for copy in sends:
        copy.wait_send()


def per_device(dps, ctxs, inputs, doc_start, gate_weight, gate_bias, decay_rate, cotangent):
    batch_rows, rows, width = inputs.shape
    hd, heads, hm = gate_weight.shape
    count = dps * ctxs
    f32, bf16 = jnp.float32, jnp.bfloat16
    part = hd // count
    full = pltpu.VMEM((rows, width), f32)
    half = pltpu.VMEM((rows, width), bf16)
    vmem = pl.BlockSpec(memory_space=pltpu.VMEM)
    out, gx, gw = pl.pallas_call(
        functools.partial(kernel, dps, ctxs),
        out_shape=(
            jax.ShapeDtypeStruct((rows, width), bf16),
            jax.ShapeDtypeStruct((rows, width), bf16),
            jax.ShapeDtypeStruct((heads, part, hm), f32),
        ),
        in_specs=[vmem] * 6,
        out_specs=(vmem,) * 3,
        scratch_shapes=[
            full, half, pltpu.VMEM((width, rows), bf16), full, pltpu.VMEM((rows, hm), f32),
            full, full, full, full, full, full, full, full, full,
            half, pltpu.VMEM((rows, heads * hm), bf16), full,
            pltpu.VMEM((2, 2 * (width // 128), 128), f32),
            pltpu.VMEM((count - 1, 2 * (width // 128), 128), f32),
            pltpu.VMEM((heads, dps, ctxs, part, hm), f32),
            pltpu.VMEM((heads, dps - 1, ctxs, part, hm), f32),
            pltpu.VMEM((heads, ctxs - 1, part, hm), f32),
            pltpu.VMEM((heads, ctxs - 1, part, hm), f32),
            pltpu.SemaphoreType.DMA((count - 1,)),
            pltpu.SemaphoreType.DMA((count - 1,)),
            pltpu.SemaphoreType.DMA((heads, dps - 1, ctxs)),
            pltpu.SemaphoreType.DMA((heads, dps - 1, ctxs)),
            pltpu.SemaphoreType.DMA((heads, ctxs - 1)),
            pltpu.SemaphoreType.DMA((heads, ctxs - 1)),
        ],
        compiler_params=pltpu.CompilerParams(
            collective_id=0, has_side_effects=True, vmem_limit_bytes=32 * 1024 * 1024
        ),
    )(
        inputs.reshape(rows, width), doc_start.reshape(1, rows),
        jnp.transpose(gate_weight, (1, 0, 2)), gate_bias, decay_rate.reshape(1, width),
        cotangent.reshape(rows, width),
    )
    return (
        out.reshape(batch_rows, rows, width), gx.reshape(batch_rows, rows, width),
        jnp.transpose(gw, (1, 0, 2)),
    )


def solution(mesh):
    in_specs = (
        P(None, ("dp", "ctx"), "mp"),
        P(None, ("dp", "ctx")),
        P(None, "mp", None),
        P("mp", None),
        P("mp"),
        P(None, ("dp", "ctx"), "mp"),
    )
    out_specs = (
        P(None, ("dp", "ctx"), "mp"),
        P(None, ("dp", "ctx"), "mp"),
        P(("dp", "ctx"), "mp", None),
    )
    return jax.shard_map(
        functools.partial(per_device, mesh.shape["dp"], mesh.shape["ctx"]),
        mesh=mesh, in_specs=in_specs, out_specs=out_specs, check_vma=False,
    )
```

```python
import functools

import jax
import jax.numpy as jnp
from jax import lax
from jax.experimental import pallas as pl
from jax.experimental.pallas import tpu as pltpu
from jax.sharding import PartitionSpec as P

MESH = pl.DeviceIdType.MESH
SUB = 8


def kernel(
    dps, ctxs, x_hbm, doc_hbm, w_hbm, bias_hbm, rate_hbm, g_hbm, out_hbm, gx_hbm, gw_hbm,
    x_ref, doc_ref, w_pairs, bias_ref, rate_ref, g_ref, w_ref, loaded, gw_sum,
    out_ref, gx_ref, gw_ref, stored,
    xf, xb, xt, gf, pre, carry_s, s_s, p_s, la_s, q_s, c1a_s, c1b_s, c2_s, c3_s, outp, dpre,
    gxp, sums, sums_in, gwp, recv1, sbuf, recv2,
    sum_send, sum_recv, one_send, one_recv, two_send, two_recv,
):
    rows, width = x_ref.shape
    heads, hd, hm = w_ref.shape
    loads = [
        pltpu.make_async_copy(source, target, loaded.at[k])
        for k, (source, target) in enumerate((
            (x_hbm, x_ref), (doc_hbm, doc_ref), (w_hbm, w_pairs), (bias_hbm, bias_ref),
            (rate_hbm, rate_ref), (g_hbm, g_ref),
        ))
    ]
    for load in loads:
        load.start()
    count = dps * ctxs
    steps = rows // SUB
    my_dp, my_ctx = lax.axis_index("dp"), lax.axis_index("ctx")
    me = my_dp * ctxs + my_ctx
    f32, bf16 = jnp.float32, jnp.bfloat16

    barrier = pltpu.get_barrier_semaphore()
    for d in range(1, count):
        to = lax.rem(me + d, count)
        pl.semaphore_signal(
            barrier, inc=1, device_id={"dp": to // ctxs, "ctx": lax.rem(to, ctxs)},
            device_id_type=MESH,
        )

    row = lax.broadcasted_iota(jnp.int32, (rows, rows), 0)
    col = lax.broadcasted_iota(jnp.int32, (rows, rows), 1)
    here = (row % SUB) * steps + row // SUB == col
    back_here = (col % SUB) * steps + col // SUB == row
    perm = jnp.where(here, 1.0, 0.0).astype(bf16)
    unperm = jnp.where(back_here, 1.0, 0.0).astype(bf16)
    wide_row = lax.broadcasted_iota(jnp.int32, (hd, heads * hd), 0)
    wide_col = lax.broadcasted_iota(jnp.int32, (hd, heads * hd), 1)
    spread = [
        jnp.where(wide_row * heads + h == wide_col, 1.0, 0.0).astype(bf16) for h in range(heads)
    ]
    loads[0].wait()
    loads[1].wait()
    keep_col = 1.0 - jnp.sum(
        jnp.where(here, doc_ref[...].astype(f32), 0.0), axis=1, keepdims=True
    )
    xf[...] = jnp.dot(perm, x_ref[...], preferred_element_type=f32)
    xb[...] = xf[...].astype(bf16)
    spread_x = [
        jnp.dot(xb[:, h * hd : (h + 1) * hd], spread[h], preferred_element_type=f32).astype(bf16)
        for h in range(heads)
    ]
    for load in loads[2:]:
        load.wait()
    w_all = w_pairs[...].reshape(hd * heads, hm)
    gf[...] = jnp.dot(perm, g_ref[...], preferred_element_type=f32)
    chunk = lax.broadcasted_iota(jnp.int32, (SUB, hd), 0)

    ends = []
    for h in range(heads):
        ch = slice(h * hd, (h + 1) * hd)
        pre[...] = (
            jnp.dot(spread_x[h], w_all, preferred_element_type=f32) + bias_ref[h : h + 1, :]
        )
        rate8 = -8.0 * rate_ref[:, ch]
        state = prod = None
        for i in range(steps):
            rs = slice(i * SUB, (i + 1) * SUB)
            x = xf[rs, ch]
            keep = jnp.broadcast_to(keep_col[rs], (SUB, hd))
            kept = keep > 0.5
            rgate = 0.5 * jnp.tanh(0.5 * pre[rs, :hd]) + 0.5
            igate = 0.5 * jnp.tanh(0.5 * pre[rs, hd:]) + 0.5
            decay = jnp.exp(rate8 * rgate)
            square = decay * decay
            inside = 1.0 - square + 0.01
            inverse = lax.rsqrt(inside)
            carry = decay * keep
            scale = jnp.where(kept, inside * inverse, 1.0)
            c3 = scale * igate
            gated = igate * x
            drive = scale * gated
            c1 = rate8 * rgate * (1.0 - rgate)
            carry_s[rs, ch] = carry
            c1a_s[rs, ch] = carry * c1
            c1b_s[rs, ch] = gated * jnp.where(kept, -square * inverse, 0.0) * c1
            c2_s[rs, ch] = drive * (1.0 - igate)
            c3_s[rs, ch] = c3
            if i == 0:
                state, prod = drive, carry
            else:
                state, prod = carry * state + drive, carry * prod
            s_s[rs, ch] = state
            p_s[rs, ch] = prod
        adj = gf[(steps - 1) * SUB :, ch]
        tail = jnp.ones((SUB, hd), f32)
        la_s[(steps - 1) * SUB :, ch] = adj
        q_s[(steps - 1) * SUB :, ch] = tail
        for i in range(steps - 2, -1, -1):
            rs = slice(i * SUB, (i + 1) * SUB)
            after = carry_s[(i + 1) * SUB : (i + 2) * SUB, ch]
            adj = gf[rs, ch] + after * adj
            tail = after * tail
            la_s[rs, ch] = adj
            q_s[rs, ch] = tail
        first = carry_s[:SUB, ch]
        fs, fp = state, prod
        bu, bp = first * adj, prod
        s = 1
        while s < SUB:
            ok = chunk >= s
            rolled_p, rolled_s = pltpu.roll(fp, s, 0), pltpu.roll(fs, s, 0)
            fs = jnp.where(ok, fp * rolled_s + fs, fs)
            fp = jnp.where(ok, fp * rolled_p, fp)
            ok = chunk < SUB - s
            rolled_p, rolled_s = pltpu.roll(bp, SUB - s, 0), pltpu.roll(bu, SUB - s, 0)
            bu = jnp.where(ok, bp * rolled_s + bu, bu)
            bp = jnp.where(ok, bp * rolled_p, bp)
            s *= 2
        for l in range(hd // 128):
            lanes = slice(l * 128, (l + 1) * 128)
            at = h * (hd // 128) + l
            half = width // 128
            sums[0, at : at + 1] = fp[SUB - 1 :, lanes]
            sums[1, at : at + 1] = fp[SUB - 1 :, lanes]
            sums[0, half + at : half + at + 1] = bu[:1, lanes]
            sums[1, half + at : half + at + 1] = fs[SUB - 1 :, lanes]
        ends.append((
            jnp.where(chunk >= 1, pltpu.roll(fp, 1, 0), 1.0),
            jnp.where(chunk >= 1, pltpu.roll(fs, 1, 0), 0.0),
            jnp.where(chunk < SUB - 1, pltpu.roll(bp, SUB - 1, 0), 1.0),
            jnp.where(chunk < SUB - 1, pltpu.roll(bu, SUB - 1, 0), 0.0),
        ))

    pl.semaphore_wait(barrier, count - 1)
    sends = []
    summaries = []
    for d in range(1, count):
        to = lax.rem(me + d, count)
        copy = pltpu.make_async_remote_copy(
            src_ref=sums.at[(to - me + count) // count],
            dst_ref=sums_in.at[d - 1],
            send_sem=sum_send.at[d - 1],
            recv_sem=sum_recv.at[d - 1],
            device_id={"dp": to // ctxs, "ctx": lax.rem(to, ctxs)},
            device_id_type=MESH,
        )
        copy.start()
        sends.append(copy)
        summaries.append(copy)

    for h in range(heads):
        ch = slice(h * hd, (h + 1) * hd)
        xt[ch, :] = jnp.transpose(xf[:, ch]).astype(bf16)
        w_ref[h] = jnp.dot(spread[h], w_all, preferred_element_type=f32).astype(bf16)

    for copy in summaries:
        copy.wait_recv()
    half = width // 128
    state_in = jnp.zeros((half, 128), f32)
    adj_in = jnp.zeros((half, 128), f32)
    for d in range(count - 1, 0, -1):
        longer = sums_in[d - 1, :half] * state_in + sums_in[d - 1, half:]
        state_in = jnp.where(d <= me, longer, state_in)
        after = count - d - 1
        longer = sums_in[after, :half] * adj_in + sums_in[after, half:]
        adj_in = jnp.where(me + d < count, longer, adj_in)

    def lanes_of(value, h):
        per = hd // 128
        return jnp.concatenate([value[h * per + l : h * per + l + 1] for l in range(per)], axis=1)

    block = ctxs * (hd // count)
    stage_one = {}
    for h in range(heads):
        ch = slice(h * hd, (h + 1) * hd)
        ex_p, ex_s, ex_q, ex_u = ends[h]
        start = ex_s + ex_p * lanes_of(state_in, h)
        prev = start
        enter = ex_u + ex_q * lanes_of(adj_in, h)
        for i in range(0, steps, 2):
            got = []
            for j in (i, i + 1):
                rs = slice(j * SUB, (j + 1) * SUB)
                state = s_s[rs, ch] + p_s[rs, ch] * start
                adj = la_s[rs, ch] + q_s[rs, ch] * enter
                dgate = adj * (c1a_s[rs, ch] * prev + c1b_s[rs, ch])
                got.append((state, dgate, adj * c2_s[rs, ch], adj * c3_s[rs, ch]))
                prev = state
            both = slice(i * SUB, (i + 2) * SUB)
            outp[both, ch] = jnp.concatenate([got[0][0], got[1][0]]).astype(bf16)
            dpre[both, h * hm : h * hm + hd] = jnp.concatenate([got[0][1], got[1][1]]).astype(bf16)
            dpre[both, h * hm + hd : (h + 1) * hm] = jnp.concatenate(
                [got[0][2], got[1][2]]
            ).astype(bf16)
            gxp[both, ch] = jnp.concatenate([got[0][3], got[1][3]])
        for d in list(range(1, dps)) + [0]:
            to_dp = lax.rem(my_dp + d, dps)
            left = xt[pl.ds(pl.multiple_of(h * hd + to_dp * block, block), block), :]
            part = jnp.dot(left, dpre[:, h * hm : (h + 1) * hm], preferred_element_type=f32)
            gwp[h, to_dp] = part.reshape(ctxs, hd // count, hm)
            if d == 0:
                continue
            for c in list(range(1, ctxs)) + [0]:
                to_ctx = lax.rem(my_ctx + c, ctxs)
                copy = pltpu.make_async_remote_copy(
                    src_ref=gwp.at[h, to_dp, to_ctx],
                    dst_ref=recv1.at[h, d - 1, c],
                    send_sem=one_send.at[h, d - 1, c],
                    recv_sem=one_recv.at[h, d - 1, c],
                    device_id={"dp": to_dp},
                    device_id_type=MESH,
                )
                copy.start()
                sends.append(copy)
                stage_one[h, d, c] = copy

    def finish(h):
        ch = slice(h * hd, (h + 1) * hd)
        back = lax.dot_general(
            dpre[:, h * hm : (h + 1) * hm], w_ref[h], (((1,), (1,)), ((), ())),
            preferred_element_type=f32,
        )
        whole = (gxp[:, ch] + back).astype(bf16)
        gx_ref[:, ch] = jnp.dot(unperm, whole, preferred_element_type=f32).astype(bf16)
        out_ref[:, ch] = jnp.dot(unperm, outp[:, ch], preferred_element_type=f32).astype(bf16)

    for h in range(heads):
        finish(h)
    stores = [
        pltpu.make_async_copy(source, target, stored.at[k])
        for k, (source, target) in enumerate(
            ((out_ref, out_hbm), (gx_ref, gx_hbm), (gw_ref, gw_hbm))
        )
    ]
    stores[0].start()
    stores[1].start()

    stage_two = {}
    for h in range(heads):
        for c in list(range(1, ctxs)) + [0]:
            to_ctx = lax.rem(my_ctx + c, ctxs)
            total = gwp[h, my_dp, to_ctx]
            for d in range(1, dps):
                stage_one[h, d, c].wait_recv()
                total = total + recv1[h, d - 1, c]
            if c == 0:
                gw_sum[h] = total
                continue
            sbuf[h, c - 1] = total
            copy = pltpu.make_async_remote_copy(
                src_ref=sbuf.at[h, c - 1],
                dst_ref=recv2.at[h, c - 1],
                send_sem=two_send.at[h, c - 1],
                recv_sem=two_recv.at[h, c - 1],
                device_id={"ctx": to_ctx},
                device_id_type=MESH,
            )
            copy.start()
            sends.append(copy)
            stage_two[h, c] = copy
    for h in range(heads):
        total = gw_sum[h]
        for c in range(1, ctxs):
            stage_two[h, c].wait_recv()
            total = total + recv2[h, c - 1]
        gw_ref[:, h, :] = total
    stores[2].start()
    for store in stores:
        store.wait()
    for copy in sends:
        copy.wait_send()


def write_out(out_ref, gx_ref, gw_ref, out_hbm, gx_hbm, gw_hbm, done):
    copies = [
        pltpu.make_async_copy(source, target, done.at[k])
        for k, (source, target) in enumerate(
            ((out_ref, out_hbm), (gx_ref, gx_hbm), (gw_ref, gw_hbm))
        )
    ]
    for copy in copies:
        copy.start()
    for copy in copies:
        copy.wait()


def per_device(dps, ctxs, inputs, doc_start, gate_weight, gate_bias, decay_rate, cotangent):
    batch_rows, rows, width = inputs.shape
    hd, heads, hm = gate_weight.shape
    count = dps * ctxs
    f32, bf16 = jnp.float32, jnp.bfloat16
    part = hd // count
    full = pltpu.VMEM((rows, width), f32)
    half = pltpu.VMEM((rows, width), bf16)
    hbm = pl.BlockSpec(memory_space=pltpu.HBM)
    shapes = (
        jax.ShapeDtypeStruct((rows, width), bf16),
        jax.ShapeDtypeStruct((rows, width), bf16),
        jax.ShapeDtypeStruct((part, heads, hm), f32),
    )
    held = pl.pallas_call(
        functools.partial(kernel, dps, ctxs),
        out_shape=shapes,
        in_specs=[hbm] * 6,
        out_specs=(hbm,) * 3,
        scratch_shapes=[
            half, pltpu.VMEM((1, rows), jnp.int32), pltpu.VMEM((hd, heads, hm), bf16),
            pltpu.VMEM((heads, hm), f32), pltpu.VMEM((1, width), f32), half,
            pltpu.VMEM((heads, hd, hm), bf16), pltpu.SemaphoreType.DMA((6,)),
            pltpu.VMEM((heads, part, hm), f32), half, half, pltpu.VMEM((part, heads, hm), f32),
            pltpu.SemaphoreType.DMA((3,)),
            full, half, pltpu.VMEM((width, rows), bf16), full, pltpu.VMEM((rows, hm), f32),
            full, full, full, full, full, full, full, full, full,
            half, pltpu.VMEM((rows, heads * hm), bf16), full,
            pltpu.VMEM((2, 2 * (width // 128), 128), f32),
            pltpu.VMEM((count - 1, 2 * (width // 128), 128), f32),
            pltpu.VMEM((heads, dps, ctxs, part, hm), f32),
            pltpu.VMEM((heads, dps - 1, ctxs, part, hm), f32),
            pltpu.VMEM((heads, ctxs - 1, part, hm), f32),
            pltpu.VMEM((heads, ctxs - 1, part, hm), f32),
            pltpu.SemaphoreType.DMA((count - 1,)),
            pltpu.SemaphoreType.DMA((count - 1,)),
            pltpu.SemaphoreType.DMA((heads, dps - 1, ctxs)),
            pltpu.SemaphoreType.DMA((heads, dps - 1, ctxs)),
            pltpu.SemaphoreType.DMA((heads, ctxs - 1)),
            pltpu.SemaphoreType.DMA((heads, ctxs - 1)),
        ],
        compiler_params=pltpu.CompilerParams(
            collective_id=0, has_side_effects=True, vmem_limit_bytes=60 * 1024 * 1024
        ),
    )(
        inputs.reshape(rows, width), doc_start.reshape(1, rows),
        gate_weight, gate_bias, decay_rate.reshape(1, width),
        cotangent.reshape(rows, width),
    )
    out, gx, gw = pl.pallas_call(
        write_out,
        out_shape=shapes,
        in_specs=[hbm] * 3,
        out_specs=(hbm,) * 3,
        scratch_shapes=[pltpu.SemaphoreType.DMA((3,))],
        compiler_params=pltpu.CompilerParams(vmem_limit_bytes=60 * 1024 * 1024),
    )(*held)
    return (out.reshape(batch_rows, rows, width), gx.reshape(batch_rows, rows, width), gw)


def solution(mesh):
    in_specs = (
        P(None, ("dp", "ctx"), "mp"),
        P(None, ("dp", "ctx")),
        P(None, "mp", None),
        P("mp", None),
        P("mp"),
        P(None, ("dp", "ctx"), "mp"),
    )
    out_specs = (
        P(None, ("dp", "ctx"), "mp"),
        P(None, ("dp", "ctx"), "mp"),
        P(("dp", "ctx"), "mp", None),
    )
    return jax.shard_map(
        functools.partial(per_device, mesh.shape["dp"], mesh.shape["ctx"]),
        mesh=mesh, in_specs=in_specs, out_specs=out_specs, check_vma=False,
    )
```

```python
import functools

import jax
import jax.numpy as jnp
from jax import lax
from jax.experimental import pallas as pl
from jax.experimental.pallas import tpu as pltpu
from jax.sharding import PartitionSpec as P

MESH = pl.DeviceIdType.MESH
SUB = 8


def orders(bits):
    return [()] if bits == 0 else [(f,) + o for f in (1, 0) for o in orders(bits - 1)]


def number(flips):
    return sum(f << i for i, f in enumerate(flips))


def kernel(
    dps, ctxs, early, x_hbm, doc_hbm, w_hbm, bias_hbm, rate_hbm, g_hbm, out_hbm, gx_hbm, gw_hbm,
    x_ref, doc_ref, w_pairs, bias_ref, rate_ref, g_ref, w_ref, loaded, gw_sum,
    out_ref, gx_ref, gw_ref, stored,
    x_out, g_out, doc_out, x_in, g_in, doc_in,
    xf, xb, xt, gf, pre, carry_s, s_s, p_s, la_s, q_s, c1a_s, c1b_s, c2_s, c3_s, outp, dpre,
    gxp, sums, gwp, recv1, sbuf, recv2,
    early_send, early_recv, sum_send, sum_recv, one_send, one_recv, two_send, two_recv,
):
    rows, width = x_ref.shape
    heads, hd, hm = w_ref.shape
    loads = [
        pltpu.make_async_copy(source, target, loaded.at[k])
        for k, (source, target) in enumerate((
            (x_hbm, x_ref), (doc_hbm, doc_ref), (g_hbm, g_ref), (w_hbm, w_pairs),
            (bias_hbm, bias_ref), (rate_hbm, rate_ref),
        ))
    ]
    for load in loads:
        load.start()
    count = dps * ctxs
    steps = rows // SUB
    bits = ctxs.bit_length() - 1
    my_dp, my_ctx = lax.axis_index("dp"), lax.axis_index("ctx")
    me = my_dp * ctxs + my_ctx
    f32, bf16 = jnp.float32, jnp.bfloat16
    sends = []

    barrier = pltpu.get_barrier_semaphore()
    for d in range(1, count):
        to = lax.rem(me + d, count)
        pl.semaphore_signal(
            barrier, inc=1, device_id={"dp": to // ctxs, "ctx": lax.rem(to, ctxs)},
            device_id_type=MESH,
        )

    def send(source, target, send_sem, recv_sem, device):
        copy = pltpu.make_async_remote_copy(
            src_ref=source, dst_ref=target, send_sem=send_sem, recv_sem=recv_sem,
            device_id=device, device_id_type=MESH,
        )
        copy.start()
        sends.append(copy)
        return copy

    row = lax.broadcasted_iota(jnp.int32, (rows, rows), 0)
    col = lax.broadcasted_iota(jnp.int32, (rows, rows), 1)
    here = (row % SUB) * steps + row // SUB == col
    back_here = (col % SUB) * steps + col // SUB == row
    perm = jnp.where(here, 1.0, 0.0).astype(bf16)
    unperm = jnp.where(back_here, 1.0, 0.0).astype(bf16)
    wide_row = lax.broadcasted_iota(jnp.int32, (hd, heads * hd), 0)
    wide_col = lax.broadcasted_iota(jnp.int32, (hd, heads * hd), 1)
    spread = [
        jnp.where(wide_row * heads + h == wide_col, 1.0, 0.0).astype(bf16) for h in range(heads)
    ]
    chunk = lax.broadcasted_iota(jnp.int32, (SUB, hd), 0)

    for load in loads[:3]:
        load.wait()
    doc_float = doc_ref[...].astype(f32)
    if early:
        x_out[...] = x_ref[:, : early * hd].astype(f32)
        g_out[...] = g_ref[:, : early * hd].astype(f32)
        doc_out[...] = jnp.broadcast_to(doc_float, doc_out.shape)
    pl.semaphore_wait(barrier, count - 1)
    early_copies = []
    if early:
        other = {"dp": 1 - my_dp}
        for k, (source, target) in enumerate(((doc_out, doc_in), (x_out, x_in), (g_out, g_in))):
            early_copies.append(
                send(source, target, early_send.at[k], early_recv.at[k], other)
            )

    def keep_of(doc):
        return 1.0 - jnp.sum(jnp.where(here, doc, 0.0), axis=1, keepdims=True)

    def gates(u, h, keep_col, w_all):
        ch = slice(u * hd, (u + 1) * hd)
        spread_x = jnp.dot(xb[:, ch], spread[h], preferred_element_type=f32).astype(bf16)
        pre[...] = (
            jnp.dot(spread_x, w_all, preferred_element_type=f32) + bias_ref[h : h + 1, :]
        )
        rate8 = -8.0 * rate_ref[:, h * hd : (h + 1) * hd]
        state = prod = None
        for i in range(steps):
            rs = slice(i * SUB, (i + 1) * SUB)
            x = xf[rs, ch]
            keep = jnp.broadcast_to(keep_col[rs], (SUB, hd))
            kept = keep > 0.5
            rgate = 0.5 * jnp.tanh(0.5 * pre[rs, :hd]) + 0.5
            igate = 0.5 * jnp.tanh(0.5 * pre[rs, hd:]) + 0.5
            decay = jnp.exp(rate8 * rgate)
            square = decay * decay
            inside = 1.0 - square + 0.01
            inverse = lax.rsqrt(inside)
            carry = decay * keep
            scale = jnp.where(kept, inside * inverse, 1.0)
            gated = igate * x
            drive = scale * gated
            c1 = rate8 * rgate * (1.0 - rgate)
            carry_s[rs, ch] = carry
            c1a_s[rs, ch] = carry * c1
            c1b_s[rs, ch] = gated * jnp.where(kept, -square * inverse, 0.0) * c1
            c2_s[rs, ch] = drive * (1.0 - igate)
            if u < heads:
                c3_s[rs, ch] = scale * igate
            if i == 0:
                state, prod = drive, carry
            else:
                state, prod = carry * state + drive, carry * prod
            s_s[rs, ch] = state
            p_s[rs, ch] = prod
        return state, prod

    def chunks(u, state, prod):
        ch = slice(u * hd, (u + 1) * hd)
        adj = gf[(steps - 1) * SUB :, ch]
        tail = jnp.ones((SUB, hd), f32)
        la_s[(steps - 1) * SUB :, ch] = adj
        q_s[(steps - 1) * SUB :, ch] = tail
        for i in range(steps - 2, -1, -1):
            rs = slice(i * SUB, (i + 1) * SUB)
            after = carry_s[(i + 1) * SUB : (i + 2) * SUB, ch]
            adj = gf[rs, ch] + after * adj
            tail = after * tail
            la_s[rs, ch] = adj
            q_s[rs, ch] = tail
        fs, fp = state, prod
        bu, bp = carry_s[:SUB, ch] * adj, prod
        s = 1
        while s < SUB:
            ok = chunk >= s
            rolled_p, rolled_s = pltpu.roll(fp, s, 0), pltpu.roll(fs, s, 0)
            fs = jnp.where(ok, fp * rolled_s + fs, fs)
            fp = jnp.where(ok, fp * rolled_p, fp)
            ok = chunk < SUB - s
            rolled_p, rolled_s = pltpu.roll(bp, SUB - s, 0), pltpu.roll(bu, SUB - s, 0)
            bu = jnp.where(ok, bp * rolled_s + bu, bu)
            bp = jnp.where(ok, bp * rolled_p, bp)
            s *= 2
        ends = (
            jnp.where(chunk >= 1, pltpu.roll(fp, 1, 0), 1.0),
            jnp.where(chunk >= 1, pltpu.roll(fs, 1, 0), 0.0),
            jnp.where(chunk < SUB - 1, pltpu.roll(bp, SUB - 1, 0), 1.0),
            jnp.where(chunk < SUB - 1, pltpu.roll(bu, SUB - 1, 0), 0.0),
        )
        return ends, (fp[SUB - 1 :], fs[SUB - 1 :], bu[:1])

    per = hd // 128
    half = width // 128
    keep_col = keep_of(doc_float)
    xf[:, :width] = jnp.dot(perm, x_ref[...], preferred_element_type=f32)
    xb[:, :width] = xf[:, :width].astype(bf16)
    gf[:, :width] = jnp.dot(perm, g_ref[...], preferred_element_type=f32)
    for load in loads[3:]:
        load.wait()
    w_all = w_pairs[...].reshape(hd * heads, hm)
    ends = {}
    for h in range(heads):
        ends[h], whole = chunks(h, *gates(h, h, keep_col, w_all))
        for k, value in enumerate(whole):
            for l in range(per):
                at = k * half + h * per + l
                sums[me, at : at + 1] = value[:, l * 128 : (l + 1) * 128]

    summaries = []
    for d in range(1, count):
        to = lax.rem(me + d, count)
        summaries.append(send(
            sums.at[me], sums.at[me], sum_send.at[d - 1], sum_recv.at[d - 1],
            {"dp": to // ctxs, "ctx": lax.rem(to, ctxs)},
        ))

    for h in range(heads):
        xt[h * hd : (h + 1) * hd, :] = jnp.transpose(xf[:, h * hd : (h + 1) * hd]).astype(bf16)
        w_ref[h] = jnp.dot(spread[h], w_all, preferred_element_type=f32).astype(bf16)
    if early:
        extra = slice(width, width + early * hd)
        early_copies[0].wait_recv()
        early_copies[1].wait_recv()
        keep_other = keep_of(doc_in[:1])
        xf[:, extra] = jnp.dot(perm, x_in[...].astype(bf16), preferred_element_type=f32)
        xb[:, extra] = xf[:, extra].astype(bf16)
        xt[extra, :] = jnp.transpose(xf[:, extra]).astype(bf16)
        firsts = [gates(heads + e, e, keep_other, w_all) for e in range(early)]
        early_copies[2].wait_recv()
        gf[:, extra] = jnp.dot(perm, g_in[...].astype(bf16), preferred_element_type=f32)
        for e in range(early):
            ends[heads + e], _ = chunks(heads + e, *firsts[e])

    for copy in summaries:
        copy.wait_recv()

    def entering(place):
        state_in = jnp.zeros((half, 128), f32)
        adj_in = jnp.zeros((half, 128), f32)
        for s in range(count):
            longer = sums[s, :half] * state_in + sums[s, half : 2 * half]
            state_in = jnp.where(s < place, longer, state_in)
            t = count - 1 - s
            longer = sums[t, :half] * adj_in + sums[t, 2 * half :]
            adj_in = jnp.where(t > place, longer, adj_in)
        return state_in, adj_in

    def lanes_of(value, h):
        return jnp.concatenate([value[h * per + l : h * per + l + 1] for l in range(per)], axis=1)

    def second(u, h, enter):
        ch = slice(u * hd, (u + 1) * hd)
        ex_p, ex_s, ex_q, ex_u = ends[u]
        start = ex_s + ex_p * lanes_of(enter[0], h)
        prev = start
        later = ex_u + ex_q * lanes_of(enter[1], h)
        for i in range(0, steps, 2):
            got = []
            for j in (i, i + 1):
                rs = slice(j * SUB, (j + 1) * SUB)
                state = s_s[rs, ch] + p_s[rs, ch] * start
                adj = la_s[rs, ch] + q_s[rs, ch] * later
                dgate = adj * (c1a_s[rs, ch] * prev + c1b_s[rs, ch])
                own = (state, adj * c3_s[rs, ch]) if u < heads else ()
                got.append((dgate, adj * c2_s[rs, ch]) + own)
                prev = state
            both = slice(i * SUB, (i + 2) * SUB)
            pair = [jnp.concatenate(two) for two in zip(*got)]
            dpre[both, u * hm : u * hm + hd] = pair[0].astype(bf16)
            dpre[both, u * hm + hd : (u + 1) * hm] = pair[1].astype(bf16)
            if u < heads:
                outp[both, ch] = pair[2].astype(bf16)
                gxp[both, ch] = pair[3]

    block = ctxs * (hd // count)

    def product(u, to_dp):
        left = xt[pl.ds(pl.multiple_of(u * hd + to_dp * block, block), block), :]
        return jnp.dot(left, dpre[:, u * hm : (u + 1) * hm], preferred_element_type=f32)

    def shard(flips):
        place = 0
        for i, f in enumerate(flips):
            bit = (my_ctx // (1 << i)) % 2
            place = place + (1 << i) * (1 - bit if f else bit)
        return place

    order = orders(bits)
    stage_one = {}
    stage_two = {}

    def first_stage(h):
        for d in range(1, dps):
            to_dp = lax.rem(my_dp + d, dps)
            gwp[h, to_dp] = product(h, to_dp).reshape(ctxs, hd // count, hm)
            for flips in order:
                k = number(flips)
                stage_one[h, d, k] = send(
                    gwp.at[h, to_dp, shard(flips)], recv1.at[h, d - 1, k],
                    one_send.at[h, d - 1, k], one_recv.at[h, d - 1, k], {"dp": to_dp},
                )

    def mine(h):
        part = product(h, my_dp)
        if h < early:
            part = part + product(heads + h, my_dp)
        gwp[h, my_dp] = part.reshape(ctxs, hd // count, hm)

    def slot(step, flips):
        return sum(1 << (bits - 1 - i) for i in range(step)) + number(flips[step + 1 :])

    def second_stage(h, flips):
        step = flips.index(1) if 1 in flips else bits
        total = gwp[h, my_dp, shard(flips)]
        if h >= early:
            for d in range(1, dps):
                stage_one[h, d, number(flips)].wait_recv()
                total = total + recv1[h, d - 1, number(flips)]
        for i in range(step):
            stage_two[h, slot(i, flips)].wait_recv()
            total = total + recv2[h, slot(i, flips)]
        if step == bits:
            gw_ref[:, h, :] = total
            return
        k = slot(step, flips)
        sbuf[h, k] = total
        bit = (my_ctx // (1 << step)) % 2
        stage_two[h, k] = send(
            sbuf.at[h, k], recv2.at[h, k], two_send.at[h, k], two_recv.at[h, k],
            {"ctx": my_ctx + (1 << step) * (1 - 2 * bit)},
        )

    def finish(h):
        ch = slice(h * hd, (h + 1) * hd)
        back = lax.dot_general(
            dpre[:, h * hm : (h + 1) * hm], w_ref[h], (((1,), (1,)), ((), ())),
            preferred_element_type=f32,
        )
        whole = (gxp[:, ch] + back).astype(bf16)
        gx_ref[:, ch] = jnp.dot(unperm, whole, preferred_element_type=f32).astype(bf16)
        out_ref[:, ch] = jnp.dot(unperm, outp[:, ch], preferred_element_type=f32).astype(bf16)

    enter = entering(me)
    for h in range(early, heads):
        second(h, h, enter)
        first_stage(h)
    enter_other = entering((1 - my_dp) * ctxs + my_ctx) if early else None
    for h in range(early):
        second(h, h, enter)
        second(heads + h, h, enter_other)
        mine(h)
        for flips in order[: ctxs // 2]:
            second_stage(h, flips)
    for h in range(early, heads):
        mine(h)
    for h in range(heads):
        finish(h)
    stores = [
        pltpu.make_async_copy(source, target, stored.at[k])
        for k, (source, target) in enumerate(
            ((out_ref, out_hbm), (gx_ref, gx_hbm), (gw_ref, gw_hbm))
        )
    ]
    stores[0].start()
    stores[1].start()
    for h in range(early):
        for flips in order[ctxs // 2 : -1]:
            second_stage(h, flips)
    for h in range(early, heads):
        for flips in order[:-1]:
            second_stage(h, flips)
    for h in range(heads):
        second_stage(h, order[-1])
    stores[2].start()
    for store in stores:
        store.wait()
    for copy in sends:
        copy.wait_send()


def write_out(out_in, gx_in, gw_in, out_hbm, gx_hbm, gw_hbm, out_ref, gx_ref, gw_ref, came, done):
    ins = [
        pltpu.make_async_copy(source, target, came.at[k])
        for k, (source, target) in enumerate(((out_in, out_ref), (gx_in, gx_ref), (gw_in, gw_ref)))
    ]
    outs = [
        pltpu.make_async_copy(source, target, done.at[k])
        for k, (source, target) in enumerate(
            ((out_ref, out_hbm), (gx_ref, gx_hbm), (gw_ref, gw_hbm))
        )
    ]
    for copy in ins:
        copy.start()
    for copy, after in zip(ins, outs):
        copy.wait()
        after.start()
    for copy in outs:
        copy.wait()


def per_device(dps, ctxs, inputs, doc_start, gate_weight, gate_bias, decay_rate, cotangent):
    batch_rows, rows, width = inputs.shape
    hd, heads, hm = gate_weight.shape
    count = dps * ctxs
    early = 1 if dps == 2 and heads > 1 else 0
    lent = max(early, 1) * hd
    f32, bf16 = jnp.float32, jnp.bfloat16
    part = hd // count
    full = pltpu.VMEM((rows, width + lent), f32)
    half = pltpu.VMEM((rows, width), bf16)
    sent = pltpu.VMEM((rows, lent), f32)
    lane_rows = 3 * (width // 128)
    hbm = pl.BlockSpec(memory_space=pltpu.HBM)
    params = dict(vmem_limit_bytes=60 * 1024 * 1024)
    shapes = (
        jax.ShapeDtypeStruct((rows, width), bf16),
        jax.ShapeDtypeStruct((rows, width), bf16),
        jax.ShapeDtypeStruct((part, heads, hm), f32),
    )
    held = pl.pallas_call(
        functools.partial(kernel, dps, ctxs, early),
        out_shape=shapes,
        in_specs=[hbm] * 6,
        out_specs=(hbm,) * 3,
        scratch_shapes=[
            half, pltpu.VMEM((1, rows), jnp.int32), pltpu.VMEM((hd, heads, hm), bf16),
            pltpu.VMEM((heads, hm), f32), pltpu.VMEM((1, width), f32), half,
            pltpu.VMEM((heads, hd, hm), bf16), pltpu.SemaphoreType.DMA((6,)),
            pltpu.VMEM((heads, part, hm), f32), half, half, pltpu.VMEM((part, heads, hm), f32),
            pltpu.SemaphoreType.DMA((3,)),
            sent, sent, pltpu.VMEM((SUB, rows), f32), sent, sent, pltpu.VMEM((SUB, rows), f32),
            full, pltpu.VMEM((rows, width + lent), bf16), pltpu.VMEM((width + lent, rows), bf16),
            full, pltpu.VMEM((rows, hm), f32),
            full, full, full, full, full, full, full, full, full,
            half, pltpu.VMEM((rows, (heads + max(early, 1)) * hm), bf16),
            pltpu.VMEM((rows, width), f32),
            pltpu.VMEM((count, lane_rows, 128), f32),
            pltpu.VMEM((heads, dps, ctxs, part, hm), f32),
            pltpu.VMEM((heads, dps - 1, ctxs, part, hm), f32),
            pltpu.VMEM((heads, ctxs - 1, part, hm), f32),
            pltpu.VMEM((heads, ctxs - 1, part, hm), f32),
            pltpu.SemaphoreType.DMA((3,)),
            pltpu.SemaphoreType.DMA((3,)),
            pltpu.SemaphoreType.DMA((count - 1,)),
            pltpu.SemaphoreType.DMA((count - 1,)),
            pltpu.SemaphoreType.DMA((heads, dps - 1, ctxs)),
            pltpu.SemaphoreType.DMA((heads, dps - 1, ctxs)),
            pltpu.SemaphoreType.DMA((heads, ctxs - 1)),
            pltpu.SemaphoreType.DMA((heads, ctxs - 1)),
        ],
        compiler_params=pltpu.CompilerParams(collective_id=0, has_side_effects=True, **params),
    )(
        inputs.reshape(rows, width), doc_start.reshape(1, rows), gate_weight, gate_bias,
        decay_rate.reshape(1, width), cotangent.reshape(rows, width),
    )
    out, gx, gw = pl.pallas_call(
        write_out,
        out_shape=shapes,
        in_specs=[hbm] * 3,
        out_specs=(hbm,) * 3,
        scratch_shapes=[
            half, half, pltpu.VMEM((part, heads, hm), f32),
            pltpu.SemaphoreType.DMA((3,)), pltpu.SemaphoreType.DMA((3,)),
        ],
        compiler_params=pltpu.CompilerParams(**params),
    )(*held)
    return (out.reshape(batch_rows, rows, width), gx.reshape(batch_rows, rows, width), gw)


def solution(mesh):
    in_specs = (
        P(None, ("dp", "ctx"), "mp"),
        P(None, ("dp", "ctx")),
        P(None, "mp", None),
        P("mp", None),
        P("mp"),
        P(None, ("dp", "ctx"), "mp"),
    )
    out_specs = (
        P(None, ("dp", "ctx"), "mp"),
        P(None, ("dp", "ctx"), "mp"),
        P(("dp", "ctx"), "mp", None),
    )
    return jax.shard_map(
        functools.partial(per_device, mesh.shape["dp"], mesh.shape["ctx"]),
        mesh=mesh, in_specs=in_specs, out_specs=out_specs, check_vma=False,
    )
```

```python
import functools

import jax
import jax.numpy as jnp
from jax import lax
from jax.experimental import pallas as pl
from jax.experimental.pallas import tpu as pltpu
from jax.sharding import PartitionSpec as P

MESH = pl.DeviceIdType.MESH
SUB = 8


def orders(bits):
    return [()] if bits == 0 else [(f,) + o for f in (1, 0) for o in orders(bits - 1)]


def number(flips):
    return sum(f << i for i, f in enumerate(flips))


def kernel(
    dps, ctxs, early, x_hbm, doc_hbm, w_hbm, bias_hbm, rate_hbm, g_hbm, out_hbm, gx_hbm, gw_hbm,
    x_ref, doc_ref, w_pairs, bias_ref, rate_ref, g_ref, w_ref, loaded, gw_sum,
    out_ref, gx_ref, gw_ref, stored,
    x_out, g_out, doc_out, x_in, g_in, doc_in,
    xf, xb, xt, gf, pre, carry_s, s_s, p_s, la_s, q_s, c1a_s, c1b_s, c2_s, c3_s, outp, dpre,
    gxp, sums, gwp, recv1, sbuf, recv2,
    early_send, early_recv, sum_send, sum_recv, one_send, one_recv, two_send, two_recv,
):
    rows, width = x_ref.shape
    heads, hd, hm = w_ref.shape
    loads = [
        pltpu.make_async_copy(source, target, loaded.at[k])
        for k, (source, target) in enumerate((
            (x_hbm, x_ref), (doc_hbm, doc_ref), (g_hbm, g_ref), (w_hbm, w_pairs),
            (bias_hbm, bias_ref), (rate_hbm, rate_ref),
        ))
    ]
    for load in loads:
        load.start()
    count = dps * ctxs
    steps = rows // SUB
    bits = ctxs.bit_length() - 1
    my_dp, my_ctx = lax.axis_index("dp"), lax.axis_index("ctx")
    me = my_dp * ctxs + my_ctx
    f32, bf16 = jnp.float32, jnp.bfloat16
    sends = []

    barrier = pltpu.get_barrier_semaphore()
    for d in range(1, count):
        to = lax.rem(me + d, count)
        pl.semaphore_signal(
            barrier, inc=1, device_id={"dp": to // ctxs, "ctx": lax.rem(to, ctxs)},
            device_id_type=MESH,
        )

    def send(source, target, send_sem, recv_sem, device):
        copy = pltpu.make_async_remote_copy(
            src_ref=source, dst_ref=target, send_sem=send_sem, recv_sem=recv_sem,
            device_id=device, device_id_type=MESH,
        )
        copy.start()
        sends.append(copy)
        return copy

    row = lax.broadcasted_iota(jnp.int32, (rows, rows), 0)
    col = lax.broadcasted_iota(jnp.int32, (rows, rows), 1)
    low = SUB.bit_length() - 1
    here = (row & (SUB - 1)) * steps + (row >> low) == col
    back_here = (col & (SUB - 1)) * steps + (col >> low) == row
    perm = jnp.where(here, 1.0, 0.0).astype(bf16)
    unperm = jnp.where(back_here, 1.0, 0.0).astype(bf16)
    wide_row = lax.broadcasted_iota(jnp.int32, (hd, heads * hd), 0)
    wide_col = lax.broadcasted_iota(jnp.int32, (hd, heads * hd), 1)
    spread = [
        jnp.where(wide_row * heads + h == wide_col, 1.0, 0.0).astype(bf16) for h in range(heads)
    ]
    chunk = lax.broadcasted_iota(jnp.int32, (SUB, hd), 0)

    for load in loads[:3]:
        load.wait()
    doc_float = doc_ref[...].astype(f32)
    if early:
        x_out[...] = x_ref[:, : early * hd].astype(f32)
        g_out[...] = g_ref[:, : early * hd].astype(f32)
        doc_out[...] = jnp.broadcast_to(doc_float, doc_out.shape)
    pl.semaphore_wait(barrier, count - 1)
    early_copies = []
    if early:
        other = {"dp": 1 - my_dp}
        for k, (source, target) in enumerate(((doc_out, doc_in), (x_out, x_in), (g_out, g_in))):
            early_copies.append(
                send(source, target, early_send.at[k], early_recv.at[k], other)
            )

    def keep_of(doc):
        return 1.0 - jnp.sum(jnp.where(here, doc, 0.0), axis=1, keepdims=True)

    def project(u, h, w_all):
        ch = slice(u * hd, (u + 1) * hd)
        spread_x = jnp.dot(xb[:, ch], spread[h], preferred_element_type=f32).astype(bf16)
        pre[:, u * hm : (u + 1) * hm] = (
            jnp.dot(spread_x, w_all, preferred_element_type=f32) + bias_ref[h : h + 1, :]
        )

    def gates(u, h, keep_col):
        ch = slice(u * hd, (u + 1) * hd)
        rate8 = -8.0 * rate_ref[:, h * hd : (h + 1) * hd]
        state = prod = None
        for i in range(steps):
            rs = slice(i * SUB, (i + 1) * SUB)
            x = xf[rs, ch]
            keep = jnp.broadcast_to(keep_col[rs], (SUB, hd))
            kept = keep > 0.5
            rgate = 0.5 * jnp.tanh(0.5 * pre[rs, u * hm : u * hm + hd]) + 0.5
            igate = 0.5 * jnp.tanh(0.5 * pre[rs, u * hm + hd : (u + 1) * hm]) + 0.5
            decay = jnp.exp(rate8 * rgate)
            square = decay * decay
            inside = 1.0 - square + 0.01
            inverse = lax.rsqrt(inside)
            carry = decay * keep
            scale = jnp.where(kept, inside * inverse, 1.0)
            gated = igate * x
            drive = scale * gated
            c1 = rate8 * rgate * (1.0 - rgate)
            carry_s[rs, ch] = carry
            c1a_s[rs, ch] = carry * c1
            c1b_s[rs, ch] = gated * jnp.where(kept, -square * inverse, 0.0) * c1
            c2_s[rs, ch] = drive * (1.0 - igate)
            if u < heads:
                c3_s[rs, ch] = scale * igate
            if i == 0:
                state, prod = drive, carry
            else:
                state, prod = carry * state + drive, carry * prod
            s_s[rs, ch] = state
            p_s[rs, ch] = prod
        return state, prod

    def chunks(u, state, prod):
        ch = slice(u * hd, (u + 1) * hd)
        adj = gf[(steps - 1) * SUB :, ch]
        tail = jnp.ones((SUB, hd), f32)
        la_s[(steps - 1) * SUB :, ch] = adj
        q_s[(steps - 1) * SUB :, ch] = tail
        for i in range(steps - 2, -1, -1):
            rs = slice(i * SUB, (i + 1) * SUB)
            after = carry_s[(i + 1) * SUB : (i + 2) * SUB, ch]
            adj = gf[rs, ch] + after * adj
            tail = after * tail
            la_s[rs, ch] = adj
            q_s[rs, ch] = tail
        fs, fp = state, prod
        bu, bp = carry_s[:SUB, ch] * adj, prod
        s = 1
        while s < SUB:
            ok = chunk >= s
            rolled_p, rolled_s = pltpu.roll(fp, s, 0), pltpu.roll(fs, s, 0)
            fs = jnp.where(ok, fp * rolled_s + fs, fs)
            fp = jnp.where(ok, fp * rolled_p, fp)
            ok = chunk < SUB - s
            rolled_p, rolled_s = pltpu.roll(bp, SUB - s, 0), pltpu.roll(bu, SUB - s, 0)
            bu = jnp.where(ok, bp * rolled_s + bu, bu)
            bp = jnp.where(ok, bp * rolled_p, bp)
            s *= 2
        ends = (
            jnp.where(chunk >= 1, pltpu.roll(fp, 1, 0), 1.0),
            jnp.where(chunk >= 1, pltpu.roll(fs, 1, 0), 0.0),
            jnp.where(chunk < SUB - 1, pltpu.roll(bp, SUB - 1, 0), 1.0),
            jnp.where(chunk < SUB - 1, pltpu.roll(bu, SUB - 1, 0), 0.0),
        )
        return ends, (fp[SUB - 1 :], fs[SUB - 1 :], bu[:1])

    per = hd // 128
    half = width // 128
    keep_col = keep_of(doc_float)
    xf[:, :width] = jnp.dot(perm, x_ref[...], preferred_element_type=f32)
    xb[:, :width] = xf[:, :width].astype(bf16)
    gf[:, :width] = jnp.dot(perm, g_ref[...], preferred_element_type=f32)
    for load in loads[3:]:
        load.wait()
    w_all = w_pairs[...].reshape(hd * heads, hm)
    ends = {}
    for h in range(heads):
        project(h, h, w_all)
    for h in range(heads):
        ends[h], whole = chunks(h, *gates(h, h, keep_col))
        for k, value in enumerate(whole):
            for l in range(per):
                at = k * half + h * per + l
                sums[me, at : at + 1] = value[:, l * 128 : (l + 1) * 128]

    summaries = []
    for d in range(1, count):
        to = lax.rem(me + d, count)
        summaries.append(send(
            sums.at[me], sums.at[me], sum_send.at[d - 1], sum_recv.at[d - 1],
            {"dp": to // ctxs, "ctx": lax.rem(to, ctxs)},
        ))

    for h in range(heads):
        xt[h * hd : (h + 1) * hd, :] = jnp.transpose(xf[:, h * hd : (h + 1) * hd]).astype(bf16)

    for copy in summaries:
        copy.wait_recv()

    def entering(place):
        state_in = jnp.zeros((half, 128), f32)
        adj_in = jnp.zeros((half, 128), f32)
        for s in range(count):
            longer = sums[s, :half] * state_in + sums[s, half : 2 * half]
            state_in = jnp.where(s < place, longer, state_in)
            t = count - 1 - s
            longer = sums[t, :half] * adj_in + sums[t, 2 * half :]
            adj_in = jnp.where(t > place, longer, adj_in)
        return state_in, adj_in

    def lanes_of(value, h):
        return jnp.concatenate([value[h * per + l : h * per + l + 1] for l in range(per)], axis=1)

    def second(u, h, enter):
        ch = slice(u * hd, (u + 1) * hd)
        ex_p, ex_s, ex_q, ex_u = ends[u]
        start = ex_s + ex_p * lanes_of(enter[0], h)
        prev = start
        later = ex_u + ex_q * lanes_of(enter[1], h)
        for i in range(0, steps, 2):
            got = []
            for j in (i, i + 1):
                rs = slice(j * SUB, (j + 1) * SUB)
                state = s_s[rs, ch] + p_s[rs, ch] * start
                adj = la_s[rs, ch] + q_s[rs, ch] * later
                dgate = adj * (c1a_s[rs, ch] * prev + c1b_s[rs, ch])
                own = (state, adj * c3_s[rs, ch]) if u < heads else ()
                got.append((dgate, adj * c2_s[rs, ch]) + own)
                prev = state
            both = slice(i * SUB, (i + 2) * SUB)
            pair = [jnp.concatenate(two) for two in zip(*got)]
            dpre[both, u * hm : u * hm + hd] = pair[0].astype(bf16)
            dpre[both, u * hm + hd : (u + 1) * hm] = pair[1].astype(bf16)
            if u < heads:
                outp[both, ch] = pair[2].astype(bf16)
                gxp[both, ch] = pair[3]

    block = ctxs * (hd // count)

    def product(u, to_dp):
        left = xt[pl.ds(pl.multiple_of(u * hd + to_dp * block, block), block), :]
        return jnp.dot(left, dpre[:, u * hm : (u + 1) * hm], preferred_element_type=f32)

    def shard(flips):
        place = 0
        for i, f in enumerate(flips):
            bit = (my_ctx // (1 << i)) % 2
            place = place + (1 << i) * (1 - bit if f else bit)
        return place

    order = orders(bits)
    stage_one = {}
    stage_two = {}

    def first_stage(h):
        for d in range(1, dps):
            to_dp = lax.rem(my_dp + d, dps)
            gwp[h, to_dp] = product(h, to_dp).reshape(ctxs, hd // count, hm)
            for flips in order:
                k = number(flips)
                stage_one[h, d, k] = send(
                    gwp.at[h, to_dp, shard(flips)], recv1.at[h, d - 1, k],
                    one_send.at[h, d - 1, k], one_recv.at[h, d - 1, k], {"dp": to_dp},
                )

    def mine(h):
        part = product(h, my_dp)
        if h < early:
            part = part + product(heads + h, my_dp)
        gwp[h, my_dp] = part.reshape(ctxs, hd // count, hm)

    def slot(step, flips):
        return sum(1 << (bits - 1 - i) for i in range(step)) + number(flips[step + 1 :])

    def second_stage(h, flips):
        step = flips.index(1) if 1 in flips else bits
        total = gwp[h, my_dp, shard(flips)]
        if h >= early:
            for d in range(1, dps):
                stage_one[h, d, number(flips)].wait_recv()
                total = total + recv1[h, d - 1, number(flips)]
        for i in range(step):
            stage_two[h, slot(i, flips)].wait_recv()
            total = total + recv2[h, slot(i, flips)]
        if step == bits:
            gw_ref[:, h, :] = total
            return
        k = slot(step, flips)
        sbuf[h, k] = total
        bit = (my_ctx // (1 << step)) % 2
        stage_two[h, k] = send(
            sbuf.at[h, k], recv2.at[h, k], two_send.at[h, k], two_recv.at[h, k],
            {"ctx": my_ctx + (1 << step) * (1 - 2 * bit)},
        )

    def finish(h):
        ch = slice(h * hd, (h + 1) * hd)
        back = lax.dot_general(
            dpre[:, h * hm : (h + 1) * hm], w_ref[h], (((1,), (1,)), ((), ())),
            preferred_element_type=f32,
        )
        whole = (gxp[:, ch] + back).astype(bf16)
        gx_ref[:, ch] = jnp.dot(unperm, whole, preferred_element_type=f32).astype(bf16)
        out_ref[:, ch] = jnp.dot(unperm, outp[:, ch], preferred_element_type=f32).astype(bf16)

    enter = entering(me)
    for h in range(early, heads):
        second(h, h, enter)
        first_stage(h)
    for h in range(early):
        second(h, h, enter)
    if early:
        extra = slice(width, width + early * hd)
        early_copies[0].wait_recv()
        early_copies[1].wait_recv()
        keep_other = keep_of(doc_in[:1])
        xf[:, extra] = jnp.dot(perm, x_in[...].astype(bf16), preferred_element_type=f32)
        xb[:, extra] = xf[:, extra].astype(bf16)
        xt[extra, :] = jnp.transpose(xf[:, extra]).astype(bf16)
        for e in range(early):
            project(heads + e, e, w_all)
        firsts = [gates(heads + e, e, keep_other) for e in range(early)]
        enter_other = entering((1 - my_dp) * ctxs + my_ctx)
        early_copies[2].wait_recv()
        gf[:, extra] = jnp.dot(perm, g_in[...].astype(bf16), preferred_element_type=f32)
        for e in range(early):
            ends[heads + e], _ = chunks(heads + e, *firsts[e])
            second(heads + e, e, enter_other)
            mine(e)
            for flips in order[: ctxs // 2]:
                second_stage(e, flips)
    for h in range(early, heads):
        mine(h)
    for h in range(heads):
        w_ref[h] = jnp.dot(spread[h], w_all, preferred_element_type=f32).astype(bf16)
        finish(h)
    stores = [
        pltpu.make_async_copy(source, target, stored.at[k])
        for k, (source, target) in enumerate(
            ((out_ref, out_hbm), (gx_ref, gx_hbm), (gw_ref, gw_hbm))
        )
    ]
    stores[0].start()
    stores[1].start()
    for h in range(early):
        for flips in order[ctxs // 2 : -1]:
            second_stage(h, flips)
    for h in range(early, heads):
        for flips in order[:-1]:
            second_stage(h, flips)
    for h in range(heads):
        second_stage(h, order[-1])
    stores[2].start()
    for store in stores:
        store.wait()
    for copy in sends:
        copy.wait_send()


def write_out(out_in, gx_in, gw_in, out_hbm, gx_hbm, gw_hbm, out_ref, gx_ref, gw_ref, came, done):
    ins = [
        pltpu.make_async_copy(source, target, came.at[k])
        for k, (source, target) in enumerate(((out_in, out_ref), (gx_in, gx_ref), (gw_in, gw_ref)))
    ]
    outs = [
        pltpu.make_async_copy(source, target, done.at[k])
        for k, (source, target) in enumerate(
            ((out_ref, out_hbm), (gx_ref, gx_hbm), (gw_ref, gw_hbm))
        )
    ]
    for copy in ins:
        copy.start()
    for copy, after in zip(ins, outs):
        copy.wait()
        after.start()
    for copy in outs:
        copy.wait()


def per_device(dps, ctxs, inputs, doc_start, gate_weight, gate_bias, decay_rate, cotangent):
    batch_rows, rows, width = inputs.shape
    hd, heads, hm = gate_weight.shape
    count = dps * ctxs
    early = 1 if dps == 2 and heads > 1 else 0
    lent = max(early, 1) * hd
    f32, bf16 = jnp.float32, jnp.bfloat16
    part = hd // count
    full = pltpu.VMEM((rows, width + lent), f32)
    half = pltpu.VMEM((rows, width), bf16)
    sent = pltpu.VMEM((rows, lent), f32)
    lane_rows = 3 * (width // 128)
    hbm = pl.BlockSpec(memory_space=pltpu.HBM)
    params = dict(vmem_limit_bytes=60 * 1024 * 1024)
    shapes = (
        jax.ShapeDtypeStruct((rows, width), bf16),
        jax.ShapeDtypeStruct((rows, width), bf16),
        jax.ShapeDtypeStruct((part, heads, hm), f32),
    )
    held = pl.pallas_call(
        functools.partial(kernel, dps, ctxs, early),
        out_shape=shapes,
        in_specs=[hbm] * 6,
        out_specs=(hbm,) * 3,
        scratch_shapes=[
            half, pltpu.VMEM((1, rows), jnp.int32), pltpu.VMEM((hd, heads, hm), bf16),
            pltpu.VMEM((heads, hm), f32), pltpu.VMEM((1, width), f32), half,
            pltpu.VMEM((heads, hd, hm), bf16), pltpu.SemaphoreType.DMA((6,)),
            pltpu.VMEM((heads, part, hm), f32), half, half, pltpu.VMEM((part, heads, hm), f32),
            pltpu.SemaphoreType.DMA((3,)),
            sent, sent, pltpu.VMEM((SUB, rows), f32), sent, sent, pltpu.VMEM((SUB, rows), f32),
            full, pltpu.VMEM((rows, width + lent), bf16), pltpu.VMEM((width + lent, rows), bf16),
            full, pltpu.VMEM((rows, (heads + max(early, 1)) * hm), f32),
            full, full, full, full, full, full, full, full, full,
            half, pltpu.VMEM((rows, (heads + max(early, 1)) * hm), bf16),
            pltpu.VMEM((rows, width), f32),
            pltpu.VMEM((count, lane_rows, 128), f32),
            pltpu.VMEM((heads, dps, ctxs, part, hm), f32),
            pltpu.VMEM((heads, dps - 1, ctxs, part, hm), f32),
            pltpu.VMEM((heads, ctxs - 1, part, hm), f32),
            pltpu.VMEM((heads, ctxs - 1, part, hm), f32),
            pltpu.SemaphoreType.DMA((3,)),
            pltpu.SemaphoreType.DMA((3,)),
            pltpu.SemaphoreType.DMA((count - 1,)),
            pltpu.SemaphoreType.DMA((count - 1,)),
            pltpu.SemaphoreType.DMA((heads, dps - 1, ctxs)),
            pltpu.SemaphoreType.DMA((heads, dps - 1, ctxs)),
            pltpu.SemaphoreType.DMA((heads, ctxs - 1)),
            pltpu.SemaphoreType.DMA((heads, ctxs - 1)),
        ],
        compiler_params=pltpu.CompilerParams(collective_id=0, has_side_effects=True, **params),
    )(
        inputs.reshape(rows, width), doc_start.reshape(1, rows), gate_weight, gate_bias,
        decay_rate.reshape(1, width), cotangent.reshape(rows, width),
    )
    out, gx, gw = pl.pallas_call(
        write_out,
        out_shape=shapes,
        in_specs=[hbm] * 3,
        out_specs=(hbm,) * 3,
        scratch_shapes=[
            half, half, pltpu.VMEM((part, heads, hm), f32),
            pltpu.SemaphoreType.DMA((3,)), pltpu.SemaphoreType.DMA((3,)),
        ],
        compiler_params=pltpu.CompilerParams(**params),
    )(*held)
    return (out.reshape(batch_rows, rows, width), gx.reshape(batch_rows, rows, width), gw)


def solution(mesh):
    in_specs = (
        P(None, ("dp", "ctx"), "mp"),
        P(None, ("dp", "ctx")),
        P(None, "mp", None),
        P("mp", None),
        P("mp"),
        P(None, ("dp", "ctx"), "mp"),
    )
    out_specs = (
        P(None, ("dp", "ctx"), "mp"),
        P(None, ("dp", "ctx"), "mp"),
        P(("dp", "ctx"), "mp", None),
    )
    return jax.shard_map(
        functools.partial(per_device, mesh.shape["dp"], mesh.shape["ctx"]),
        mesh=mesh, in_specs=in_specs, out_specs=out_specs, check_vma=False,
    )
```

```python
import functools

import jax
import jax.numpy as jnp
from jax import lax
from jax.experimental import pallas as pl
from jax.experimental.pallas import tpu as pltpu
from jax.sharding import PartitionSpec as P

MESH = pl.DeviceIdType.MESH
SUB = 8


def orders(bits):
    return [()] if bits == 0 else [(f,) + o for f in (1, 0) for o in orders(bits - 1)]


def number(flips):
    return sum(f << i for i, f in enumerate(flips))


def kernel(
    dps, ctxs, early, x_hbm, doc_hbm, w_hbm, bias_hbm, rate_hbm, g_hbm, out_hbm, gx_hbm, gw_hbm,
    x_ref, doc_ref, w_pairs, bias_ref, rate_ref, g_ref, w_ref, loaded, gw_sum,
    out_ref, gx_ref, gw_ref, stored,
    x_out, g_out, doc_out, x_in, g_in, doc_in,
    xf, xb, xt, gf, pre, carry_s, s_s, p_s, la_s, q_s, c1a_s, c1b_s, c2_s, c3_s, outp, dpre,
    gxp, sums, gwp, recv1, sbuf, recv2,
    early_send, early_recv, sum_send, sum_recv, one_send, one_recv, two_send, two_recv,
):
    rows, width = x_ref.shape
    heads, hd, hm = w_ref.shape
    loads = [
        pltpu.make_async_copy(source, target, loaded.at[k])
        for k, (source, target) in enumerate((
            (x_hbm, x_ref), (doc_hbm, doc_ref), (g_hbm, g_ref), (w_hbm, w_pairs),
            (bias_hbm, bias_ref), (rate_hbm, rate_ref),
        ))
    ]
    for load in loads:
        load.start()
    count = dps * ctxs
    steps = rows // SUB
    bits = ctxs.bit_length() - 1
    my_dp, my_ctx = lax.axis_index("dp"), lax.axis_index("ctx")
    me = my_dp * ctxs + my_ctx
    f32, bf16 = jnp.float32, jnp.bfloat16
    sends = []

    barrier = pltpu.get_barrier_semaphore()
    for d in range(1, count):
        to = lax.rem(me + d, count)
        pl.semaphore_signal(
            barrier, inc=1, device_id={"dp": to // ctxs, "ctx": lax.rem(to, ctxs)},
            device_id_type=MESH,
        )

    def send(source, target, send_sem, recv_sem, device):
        copy = pltpu.make_async_remote_copy(
            src_ref=source, dst_ref=target, send_sem=send_sem, recv_sem=recv_sem,
            device_id=device, device_id_type=MESH,
        )
        copy.start()
        sends.append(copy)
        return copy

    row = lax.broadcasted_iota(jnp.int32, (rows, rows), 0)
    col = lax.broadcasted_iota(jnp.int32, (rows, rows), 1)
    low = SUB.bit_length() - 1
    here = (row & (SUB - 1)) * steps + (row >> low) == col
    back_here = (col & (SUB - 1)) * steps + (col >> low) == row
    perm = jnp.where(here, 1.0, 0.0).astype(bf16)
    unperm = jnp.where(back_here, 1.0, 0.0).astype(bf16)
    wide_row = lax.broadcasted_iota(jnp.int32, (hd, heads * hd), 0)
    wide_col = lax.broadcasted_iota(jnp.int32, (hd, heads * hd), 1)
    spread = [
        jnp.where(wide_row * heads + h == wide_col, 1.0, 0.0).astype(bf16) for h in range(heads)
    ]
    chunk = lax.broadcasted_iota(jnp.int32, (SUB, hd), 0)

    for load in loads[:3]:
        load.wait()
    doc_float = doc_ref[...].astype(f32)
    if early:
        x_out[...] = x_ref[:, : early * hd].astype(f32)
        g_out[...] = g_ref[:, : early * hd].astype(f32)
        doc_out[...] = jnp.broadcast_to(doc_float, doc_out.shape)
    pl.semaphore_wait(barrier, count - 1)
    early_copies = []
    if early:
        other = {"dp": 1 - my_dp}
        for k, (source, target) in enumerate(((doc_out, doc_in), (x_out, x_in), (g_out, g_in))):
            early_copies.append(
                send(source, target, early_send.at[k], early_recv.at[k], other)
            )

    def keep_of(doc):
        return 1.0 - jnp.sum(jnp.where(here, doc, 0.0), axis=1, keepdims=True)

    def project(u, h, w_all):
        ch = slice(u * hd, (u + 1) * hd)
        spread_x = jnp.dot(xb[:, ch], spread[h], preferred_element_type=f32).astype(bf16)
        pre[:, u * hm : (u + 1) * hm] = (
            jnp.dot(spread_x, w_all, preferred_element_type=f32) + bias_ref[h : h + 1, :]
        )

    def gates(u, h, keep_col):
        ch = slice(u * hd, (u + 1) * hd)
        rate8 = -8.0 * rate_ref[:, h * hd : (h + 1) * hd]
        state = prod = None
        for i in range(steps):
            rs = slice(i * SUB, (i + 1) * SUB)
            x = xf[rs, ch]
            keep = jnp.broadcast_to(keep_col[rs], (SUB, hd))
            kept = keep > 0.5
            rgate = 0.5 * jnp.tanh(0.5 * pre[rs, u * hm : u * hm + hd]) + 0.5
            igate = 0.5 * jnp.tanh(0.5 * pre[rs, u * hm + hd : (u + 1) * hm]) + 0.5
            decay = jnp.exp(rate8 * rgate)
            square = decay * decay
            inside = 1.0 - square + 0.01
            inverse = lax.rsqrt(inside)
            carry = decay * keep
            scale = jnp.where(kept, inside * inverse, 1.0)
            gated = igate * x
            drive = scale * gated
            c1 = rate8 * rgate * (1.0 - rgate)
            carry_s[rs, ch] = carry
            c1a_s[rs, ch] = carry * c1
            c1b_s[rs, ch] = gated * jnp.where(kept, -square * inverse, 0.0) * c1
            c2_s[rs, ch] = drive * (1.0 - igate)
            if u < heads:
                c3_s[rs, ch] = scale * igate
            if i == 0:
                state, prod = drive, carry
            else:
                state, prod = carry * state + drive, carry * prod
            s_s[rs, ch] = state
            p_s[rs, ch] = prod
        return state, prod

    def chunks(u, state, prod):
        ch = slice(u * hd, (u + 1) * hd)
        adj = gf[(steps - 1) * SUB :, ch]
        tail = jnp.ones((SUB, hd), f32)
        la_s[(steps - 1) * SUB :, ch] = adj
        q_s[(steps - 1) * SUB :, ch] = tail
        for i in range(steps - 2, -1, -1):
            rs = slice(i * SUB, (i + 1) * SUB)
            after = carry_s[(i + 1) * SUB : (i + 2) * SUB, ch]
            adj = gf[rs, ch] + after * adj
            tail = after * tail
            la_s[rs, ch] = adj
            q_s[rs, ch] = tail
        fs, fp = state, prod
        bu, bp = carry_s[:SUB, ch] * adj, prod
        s = 1
        while s < SUB:
            ok = chunk >= s
            rolled_p, rolled_s = pltpu.roll(fp, s, 0), pltpu.roll(fs, s, 0)
            fs = jnp.where(ok, fp * rolled_s + fs, fs)
            fp = jnp.where(ok, fp * rolled_p, fp)
            ok = chunk < SUB - s
            rolled_p, rolled_s = pltpu.roll(bp, SUB - s, 0), pltpu.roll(bu, SUB - s, 0)
            bu = jnp.where(ok, bp * rolled_s + bu, bu)
            bp = jnp.where(ok, bp * rolled_p, bp)
            s *= 2
        ends = (
            jnp.where(chunk >= 1, pltpu.roll(fp, 1, 0), 1.0),
            jnp.where(chunk >= 1, pltpu.roll(fs, 1, 0), 0.0),
            jnp.where(chunk < SUB - 1, pltpu.roll(bp, SUB - 1, 0), 1.0),
            jnp.where(chunk < SUB - 1, pltpu.roll(bu, SUB - 1, 0), 0.0),
        )
        return ends, (fp[SUB - 1 :], fs[SUB - 1 :], bu[:1])

    per = hd // 128
    half = width // 128
    keep_col = keep_of(doc_float)
    xf[:, :width] = jnp.dot(perm, x_ref[...], preferred_element_type=f32)
    xb[:, :width] = xf[:, :width].astype(bf16)
    gf[:, :width] = jnp.dot(perm, g_ref[...], preferred_element_type=f32)
    for load in loads[3:]:
        load.wait()
    w_all = w_pairs[...].reshape(hd * heads, hm)
    ends = {}
    for h in range(heads):
        project(h, h, w_all)
    for h in range(heads):
        ends[h], whole = chunks(h, *gates(h, h, keep_col))
        for k, value in enumerate(whole):
            for l in range(per):
                at = k * half + h * per + l
                sums[me, at : at + 1] = value[:, l * 128 : (l + 1) * 128]

    summaries = []
    for d in range(1, count):
        to = lax.rem(me + d, count)
        summaries.append(send(
            sums.at[me], sums.at[me], sum_send.at[d - 1], sum_recv.at[d - 1],
            {"dp": to // ctxs, "ctx": lax.rem(to, ctxs)},
        ))

    for h in range(heads):
        xt[h * hd : (h + 1) * hd, :] = jnp.transpose(xf[:, h * hd : (h + 1) * hd]).astype(bf16)

    for h in range(heads):
        w_ref[h] = jnp.dot(spread[h], w_all, preferred_element_type=f32).astype(bf16)
    if early:
        extra = slice(width, width + early * hd)
        early_copies[0].wait_recv()
        early_copies[1].wait_recv()
        keep_other = keep_of(doc_in[:1])
        xf[:, extra] = jnp.dot(perm, x_in[...].astype(bf16), preferred_element_type=f32)
        xb[:, extra] = xf[:, extra].astype(bf16)
        xt[extra, :] = jnp.transpose(xf[:, extra]).astype(bf16)
        for e in range(early):
            project(heads + e, e, w_all)
        firsts = [gates(heads + e, e, keep_other) for e in range(early)]
        early_copies[2].wait_recv()
        gf[:, extra] = jnp.dot(perm, g_in[...].astype(bf16), preferred_element_type=f32)
        for e in range(early):
            ends[heads + e], _ = chunks(heads + e, *firsts[e])

    for copy in summaries:
        copy.wait_recv()

    def entering(place):
        state_in = jnp.zeros((half, 128), f32)
        adj_in = jnp.zeros((half, 128), f32)
        for s in range(count):
            longer = sums[s, :half] * state_in + sums[s, half : 2 * half]
            state_in = jnp.where(s < place, longer, state_in)
            t = count - 1 - s
            longer = sums[t, :half] * adj_in + sums[t, 2 * half :]
            adj_in = jnp.where(t > place, longer, adj_in)
        return state_in, adj_in

    def lanes_of(value, h):
        return jnp.concatenate([value[h * per + l : h * per + l + 1] for l in range(per)], axis=1)

    def second(u, h, enter):
        ch = slice(u * hd, (u + 1) * hd)
        ex_p, ex_s, ex_q, ex_u = ends[u]
        start = ex_s + ex_p * lanes_of(enter[0], h)
        prev = start
        later = ex_u + ex_q * lanes_of(enter[1], h)
        for i in range(0, steps, 2):
            got = []
            for j in (i, i + 1):
                rs = slice(j * SUB, (j + 1) * SUB)
                state = s_s[rs, ch] + p_s[rs, ch] * start
                adj = la_s[rs, ch] + q_s[rs, ch] * later
                dgate = adj * (c1a_s[rs, ch] * prev + c1b_s[rs, ch])
                own = (state, adj * c3_s[rs, ch]) if u < heads else ()
                got.append((dgate, adj * c2_s[rs, ch]) + own)
                prev = state
            both = slice(i * SUB, (i + 2) * SUB)
            pair = [jnp.concatenate(two) for two in zip(*got)]
            dpre[both, u * hm : u * hm + hd] = pair[0].astype(bf16)
            dpre[both, u * hm + hd : (u + 1) * hm] = pair[1].astype(bf16)
            if u < heads:
                outp[both, ch] = pair[2].astype(bf16)
                gxp[both, ch] = pair[3]

    block = ctxs * (hd // count)

    def product(u, to_dp):
        left = xt[pl.ds(pl.multiple_of(u * hd + to_dp * block, block), block), :]
        return jnp.dot(left, dpre[:, u * hm : (u + 1) * hm], preferred_element_type=f32)

    def shard(flips):
        place = 0
        for i, f in enumerate(flips):
            bit = (my_ctx // (1 << i)) % 2
            place = place + (1 << i) * (1 - bit if f else bit)
        return place

    order = orders(bits)
    stage_one = {}
    stage_two = {}

    def first_stage(h):
        for d in range(1, dps):
            to_dp = lax.rem(my_dp + d, dps)
            gwp[h, to_dp] = product(h, to_dp).reshape(ctxs, hd // count, hm)
            for flips in order:
                k = number(flips)
                stage_one[h, d, k] = send(
                    gwp.at[h, to_dp, shard(flips)], recv1.at[h, d - 1, k],
                    one_send.at[h, d - 1, k], one_recv.at[h, d - 1, k], {"dp": to_dp},
                )

    def mine(h):
        part = product(h, my_dp)
        if h < early:
            part = part + product(heads + h, my_dp)
        gwp[h, my_dp] = part.reshape(ctxs, hd // count, hm)

    def slot(step, flips):
        return sum(1 << (bits - 1 - i) for i in range(step)) + number(flips[step + 1 :])

    def second_stage(h, flips):
        step = flips.index(1) if 1 in flips else bits
        total = gwp[h, my_dp, shard(flips)]
        if h >= early:
            for d in range(1, dps):
                stage_one[h, d, number(flips)].wait_recv()
                total = total + recv1[h, d - 1, number(flips)]
        for i in range(step):
            stage_two[h, slot(i, flips)].wait_recv()
            total = total + recv2[h, slot(i, flips)]
        if step == bits:
            gw_ref[:, h, :] = total
            return
        k = slot(step, flips)
        sbuf[h, k] = total
        bit = (my_ctx // (1 << step)) % 2
        stage_two[h, k] = send(
            sbuf.at[h, k], recv2.at[h, k], two_send.at[h, k], two_recv.at[h, k],
            {"ctx": my_ctx + (1 << step) * (1 - 2 * bit)},
        )

    def finish(h):
        ch = slice(h * hd, (h + 1) * hd)
        back = lax.dot_general(
            dpre[:, h * hm : (h + 1) * hm], w_ref[h], (((1,), (1,)), ((), ())),
            preferred_element_type=f32,
        )
        whole = (gxp[:, ch] + back).astype(bf16)
        gx_ref[:, ch] = jnp.dot(unperm, whole, preferred_element_type=f32).astype(bf16)
        out_ref[:, ch] = jnp.dot(unperm, outp[:, ch], preferred_element_type=f32).astype(bf16)

    enter = entering(me)
    for h in range(early, heads):
        second(h, h, enter)
        first_stage(h)
    for h in range(early):
        second(h, h, enter)
    stores = [
        pltpu.make_async_copy(source, target, stored.at[k])
        for k, (source, target) in enumerate(
            ((out_ref, out_hbm), (gx_ref, gx_hbm), (gw_ref, gw_hbm))
        )
    ]
    enter_other = entering((1 - my_dp) * ctxs + my_ctx) if early else None
    for e in range(early):
        second(heads + e, e, enter_other)
        mine(e)
        for flips in order[: ctxs // 2]:
            second_stage(e, flips)
    for h in range(early, heads):
        mine(h)
    finish(0)
    for h in range(early, heads):
        for flips in order[: ctxs // 2]:
            second_stage(h, flips)
    for h in range(early):
        for flips in order[ctxs // 2 : -1]:
            second_stage(h, flips)
    for h in range(1, heads):
        finish(h)
    stores[0].start()
    stores[1].start()
    for h in range(early, heads):
        for flips in order[ctxs // 2 : -1]:
            second_stage(h, flips)
    for h in range(heads):
        second_stage(h, order[-1])
    stores[2].start()
    for store in stores:
        store.wait()
    for copy in sends:
        copy.wait_send()


def write_out(out_in, gx_in, gw_in, out_hbm, gx_hbm, gw_hbm, out_ref, gx_ref, gw_ref, came, done):
    ins = [
        pltpu.make_async_copy(source, target, came.at[k])
        for k, (source, target) in enumerate(((out_in, out_ref), (gx_in, gx_ref), (gw_in, gw_ref)))
    ]
    outs = [
        pltpu.make_async_copy(source, target, done.at[k])
        for k, (source, target) in enumerate(
            ((out_ref, out_hbm), (gx_ref, gx_hbm), (gw_ref, gw_hbm))
        )
    ]
    for copy in ins:
        copy.start()
    for copy, after in zip(ins, outs):
        copy.wait()
        after.start()
    for copy in outs:
        copy.wait()


def per_device(dps, ctxs, inputs, doc_start, gate_weight, gate_bias, decay_rate, cotangent):
    batch_rows, rows, width = inputs.shape
    hd, heads, hm = gate_weight.shape
    count = dps * ctxs
    early = 1 if dps == 2 and heads > 1 else 0
    lent = max(early, 1) * hd
    f32, bf16 = jnp.float32, jnp.bfloat16
    part = hd // count
    full = pltpu.VMEM((rows, width + lent), f32)
    half = pltpu.VMEM((rows, width), bf16)
    sent = pltpu.VMEM((rows, lent), f32)
    lane_rows = 3 * (width // 128)
    hbm = pl.BlockSpec(memory_space=pltpu.HBM)
    params = dict(vmem_limit_bytes=60 * 1024 * 1024)
    shapes = (
        jax.ShapeDtypeStruct((rows, width), bf16),
        jax.ShapeDtypeStruct((rows, width), bf16),
        jax.ShapeDtypeStruct((part, heads, hm), f32),
    )
    held = pl.pallas_call(
        functools.partial(kernel, dps, ctxs, early),
        out_shape=shapes,
        in_specs=[hbm] * 6,
        out_specs=(hbm,) * 3,
        scratch_shapes=[
            half, pltpu.VMEM((1, rows), jnp.int32), pltpu.VMEM((hd, heads, hm), bf16),
            pltpu.VMEM((heads, hm), f32), pltpu.VMEM((1, width), f32), half,
            pltpu.VMEM((heads, hd, hm), bf16), pltpu.SemaphoreType.DMA((6,)),
            pltpu.VMEM((heads, part, hm), f32), half, half, pltpu.VMEM((part, heads, hm), f32),
            pltpu.SemaphoreType.DMA((3,)),
            sent, sent, pltpu.VMEM((SUB, rows), f32), sent, sent, pltpu.VMEM((SUB, rows), f32),
            full, pltpu.VMEM((rows, width + lent), bf16), pltpu.VMEM((width + lent, rows), bf16),
            full, pltpu.VMEM((rows, (heads + max(early, 1)) * hm), f32),
            full, full, full, full, full, full, full, full, full,
            half, pltpu.VMEM((rows, (heads + max(early, 1)) * hm), bf16),
            pltpu.VMEM((rows, width), f32),
            pltpu.VMEM((count, lane_rows, 128), f32),
            pltpu.VMEM((heads, dps, ctxs, part, hm), f32),
            pltpu.VMEM((heads, dps - 1, ctxs, part, hm), f32),
            pltpu.VMEM((heads, ctxs - 1, part, hm), f32),
            pltpu.VMEM((heads, ctxs - 1, part, hm), f32),
            pltpu.SemaphoreType.DMA((3,)),
            pltpu.SemaphoreType.DMA((3,)),
            pltpu.SemaphoreType.DMA((count - 1,)),
            pltpu.SemaphoreType.DMA((count - 1,)),
            pltpu.SemaphoreType.DMA((heads, dps - 1, ctxs)),
            pltpu.SemaphoreType.DMA((heads, dps - 1, ctxs)),
            pltpu.SemaphoreType.DMA((heads, ctxs - 1)),
            pltpu.SemaphoreType.DMA((heads, ctxs - 1)),
        ],
        compiler_params=pltpu.CompilerParams(collective_id=0, has_side_effects=True, **params),
    )(
        inputs.reshape(rows, width), doc_start.reshape(1, rows), gate_weight, gate_bias,
        decay_rate.reshape(1, width), cotangent.reshape(rows, width),
    )
    out, gx, gw = pl.pallas_call(
        write_out,
        out_shape=shapes,
        in_specs=[hbm] * 3,
        out_specs=(hbm,) * 3,
        scratch_shapes=[
            half, half, pltpu.VMEM((part, heads, hm), f32),
            pltpu.SemaphoreType.DMA((3,)), pltpu.SemaphoreType.DMA((3,)),
        ],
        compiler_params=pltpu.CompilerParams(**params),
    )(*held)
    return (out.reshape(batch_rows, rows, width), gx.reshape(batch_rows, rows, width), gw)


def solution(mesh):
    in_specs = (
        P(None, ("dp", "ctx"), "mp"),
        P(None, ("dp", "ctx")),
        P(None, "mp", None),
        P("mp", None),
        P("mp"),
        P(None, ("dp", "ctx"), "mp"),
    )
    out_specs = (
        P(None, ("dp", "ctx"), "mp"),
        P(None, ("dp", "ctx"), "mp"),
        P(("dp", "ctx"), "mp", None),
    )
    return jax.shard_map(
        functools.partial(per_device, mesh.shape["dp"], mesh.shape["ctx"]),
        mesh=mesh, in_specs=in_specs, out_specs=out_specs, check_vma=False,
    )
```

```python
import functools

import jax
import jax.numpy as jnp
from jax import lax
from jax.experimental import pallas as pl
from jax.experimental.pallas import tpu as pltpu
from jax.sharding import PartitionSpec as P

MESH = pl.DeviceIdType.MESH
SUB = 8


def orders(bits):
    return [()] if bits == 0 else [(f,) + o for f in (1, 0) for o in orders(bits - 1)]


def number(flips):
    return sum(f << i for i, f in enumerate(flips))


def kernel(
    dps, ctxs, early, x_hbm, doc_hbm, w_hbm, bias_hbm, rate_hbm, g_hbm, out_hbm, gx_hbm, gw_hbm,
    x_ref, doc_ref, w_pairs, bias_ref, rate_ref, g_ref, w_ref, loaded, gw_sum,
    out_ref, gx_ref, gw_ref, stored,
    x_out, g_out, doc_out, x_in, g_in, doc_in, ends_in,
    xf, xb, xt, gf, pre, carry_s, s_s, p_s, la_s, q_s, c1a_s, c1b_s, c2_s, c3_s, outp, dpre,
    gxp, sums, gwp, recv1, sbuf, recv2,
    early_send, early_recv, sum_send, sum_recv, one_send, one_recv, two_send, two_recv,
):
    rows, width = x_ref.shape
    heads, hd, hm = w_ref.shape
    loads = [
        pltpu.make_async_copy(source, target, loaded.at[k])
        for k, (source, target) in enumerate((
            (x_hbm, x_ref), (doc_hbm, doc_ref), (g_hbm, g_ref), (w_hbm, w_pairs),
            (bias_hbm, bias_ref), (rate_hbm, rate_ref),
        ))
    ]
    for load in loads:
        load.start()
    count = dps * ctxs
    steps = rows // SUB
    bits = ctxs.bit_length() - 1
    lend = lax.rem(lax.axis_index("mp"), 2) == 0
    keeps = jnp.logical_not(lend)
    my_dp, my_ctx = lax.axis_index("dp"), lax.axis_index("ctx")
    me = my_dp * ctxs + my_ctx
    f32, bf16 = jnp.float32, jnp.bfloat16
    sends = []

    barrier = pltpu.get_barrier_semaphore()
    for d in range(1, count):
        to = lax.rem(me + d, count)
        pl.semaphore_signal(
            barrier, inc=1, device_id={"dp": to // ctxs, "ctx": lax.rem(to, ctxs)},
            device_id_type=MESH,
        )

    def describe(source, target, send_sem, recv_sem, device):
        return pltpu.make_async_remote_copy(
            src_ref=source, dst_ref=target, send_sem=send_sem, recv_sem=recv_sem,
            device_id=device, device_id_type=MESH,
        )

    def send(*what):
        copy = describe(*what)
        copy.start()
        sends.append(copy)
        return copy

    row = lax.broadcasted_iota(jnp.int32, (rows, rows), 0)
    col = lax.broadcasted_iota(jnp.int32, (rows, rows), 1)
    low = SUB.bit_length() - 1
    here = (row & (SUB - 1)) * steps + (row >> low) == col
    back_here = (col & (SUB - 1)) * steps + (col >> low) == row
    perm = jnp.where(here, 1.0, 0.0).astype(bf16)
    unperm = jnp.where(back_here, 1.0, 0.0).astype(bf16)
    wide_row = lax.broadcasted_iota(jnp.int32, (hd, heads * hd), 0)
    wide_col = lax.broadcasted_iota(jnp.int32, (hd, heads * hd), 1)
    spread = [
        jnp.where(wide_row * heads + h == wide_col, 1.0, 0.0).astype(bf16) for h in range(heads)
    ]
    chunk = lax.broadcasted_iota(jnp.int32, (SUB, hd), 0)

    for load in loads[:3]:
        load.wait()
    doc_float = doc_ref[...].astype(f32)
    if early:
        x_out[...] = x_ref[:, : early * hd].astype(f32)
        g_out[...] = g_ref[:, : early * hd].astype(f32)
        doc_out[...] = jnp.broadcast_to(doc_float, doc_out.shape)
    pl.semaphore_wait(barrier, count - 1)
    early_copies = [
        describe(source, target, early_send.at[k], early_recv.at[k], {"dp": 1 - my_dp})
        for k, (source, target) in enumerate(((doc_out, doc_in), (x_out, x_in), (g_out, g_in)))
    ] if early else []
    if early:

        @pl.when(lend)
        def _():
            for copy in early_copies:
                copy.start()


    def keep_of(doc):
        return 1.0 - jnp.sum(jnp.where(here, doc, 0.0), axis=1, keepdims=True)

    def project(u, h, w_all):
        ch = slice(u * hd, (u + 1) * hd)
        spread_x = jnp.dot(xb[:, ch], spread[h], preferred_element_type=f32).astype(bf16)
        pre[:, u * hm : (u + 1) * hm] = (
            jnp.dot(spread_x, w_all, preferred_element_type=f32) + bias_ref[h : h + 1, :]
        )

    def gates(u, h, keep_col):
        ch = slice(u * hd, (u + 1) * hd)
        rate8 = -8.0 * rate_ref[:, h * hd : (h + 1) * hd]
        state = prod = None
        for i in range(steps):
            rs = slice(i * SUB, (i + 1) * SUB)
            x = xf[rs, ch]
            keep = jnp.broadcast_to(keep_col[rs], (SUB, hd))
            kept = keep > 0.5
            rgate = 0.5 * jnp.tanh(0.5 * pre[rs, u * hm : u * hm + hd]) + 0.5
            igate = 0.5 * jnp.tanh(0.5 * pre[rs, u * hm + hd : (u + 1) * hm]) + 0.5
            decay = jnp.exp(rate8 * rgate)
            square = decay * decay
            inside = 1.0 - square + 0.01
            inverse = lax.rsqrt(inside)
            carry = decay * keep
            scale = jnp.where(kept, inside * inverse, 1.0)
            gated = igate * x
            drive = scale * gated
            c1 = rate8 * rgate * (1.0 - rgate)
            carry_s[rs, ch] = carry
            c1a_s[rs, ch] = carry * c1
            c1b_s[rs, ch] = gated * jnp.where(kept, -square * inverse, 0.0) * c1
            c2_s[rs, ch] = drive * (1.0 - igate)
            if u < heads:
                c3_s[rs, ch] = scale * igate
            if i == 0:
                state, prod = drive, carry
            else:
                state, prod = carry * state + drive, carry * prod
            s_s[rs, ch] = state
            p_s[rs, ch] = prod
        return state, prod

    def chunks(u, state, prod):
        ch = slice(u * hd, (u + 1) * hd)
        adj = gf[(steps - 1) * SUB :, ch]
        tail = jnp.ones((SUB, hd), f32)
        la_s[(steps - 1) * SUB :, ch] = adj
        q_s[(steps - 1) * SUB :, ch] = tail
        for i in range(steps - 2, -1, -1):
            rs = slice(i * SUB, (i + 1) * SUB)
            after = carry_s[(i + 1) * SUB : (i + 2) * SUB, ch]
            adj = gf[rs, ch] + after * adj
            tail = after * tail
            la_s[rs, ch] = adj
            q_s[rs, ch] = tail
        fs, fp = state, prod
        bu, bp = carry_s[:SUB, ch] * adj, prod
        s = 1
        while s < SUB:
            ok = chunk >= s
            rolled_p, rolled_s = pltpu.roll(fp, s, 0), pltpu.roll(fs, s, 0)
            fs = jnp.where(ok, fp * rolled_s + fs, fs)
            fp = jnp.where(ok, fp * rolled_p, fp)
            ok = chunk < SUB - s
            rolled_p, rolled_s = pltpu.roll(bp, SUB - s, 0), pltpu.roll(bu, SUB - s, 0)
            bu = jnp.where(ok, bp * rolled_s + bu, bu)
            bp = jnp.where(ok, bp * rolled_p, bp)
            s *= 2
        ends = (
            jnp.where(chunk >= 1, pltpu.roll(fp, 1, 0), 1.0),
            jnp.where(chunk >= 1, pltpu.roll(fs, 1, 0), 0.0),
            jnp.where(chunk < SUB - 1, pltpu.roll(bp, SUB - 1, 0), 1.0),
            jnp.where(chunk < SUB - 1, pltpu.roll(bu, SUB - 1, 0), 0.0),
        )
        return ends, (fp[SUB - 1 :], fs[SUB - 1 :], bu[:1])

    per = hd // 128
    half = width // 128
    keep_col = keep_of(doc_float)
    xf[:, :width] = jnp.dot(perm, x_ref[...], preferred_element_type=f32)
    xb[:, :width] = xf[:, :width].astype(bf16)
    gf[:, :width] = jnp.dot(perm, g_ref[...], preferred_element_type=f32)
    for load in loads[3:]:
        load.wait()
    w_all = w_pairs[...].reshape(hd * heads, hm)
    ends = {}
    for h in range(heads):
        project(h, h, w_all)
    for h in range(heads):
        ends[h], whole = chunks(h, *gates(h, h, keep_col))
        for k, value in enumerate(whole):
            for l in range(per):
                at = k * half + h * per + l
                sums[me, at : at + 1] = value[:, l * 128 : (l + 1) * 128]

    summaries = []
    for d in range(1, count):
        to = lax.rem(me + d, count)
        summaries.append(send(
            sums.at[me], sums.at[me], sum_send.at[d - 1], sum_recv.at[d - 1],
            {"dp": to // ctxs, "ctx": lax.rem(to, ctxs)},
        ))

    for h in range(heads):
        xt[h * hd : (h + 1) * hd, :] = jnp.transpose(xf[:, h * hd : (h + 1) * hd]).astype(bf16)

    for h in range(heads):
        w_ref[h] = jnp.dot(spread[h], w_all, preferred_element_type=f32).astype(bf16)
    if early:

        @pl.when(lend)
        def _():
            extra = slice(width, width + early * hd)
            early_copies[0].wait_recv()
            early_copies[1].wait_recv()
            keep_other = keep_of(doc_in[:1])
            xf[:, extra] = jnp.dot(perm, x_in[...].astype(bf16), preferred_element_type=f32)
            xb[:, extra] = xf[:, extra].astype(bf16)
            xt[extra, :] = jnp.transpose(xf[:, extra]).astype(bf16)
            for e in range(early):
                project(heads + e, e, w_all)
            firsts = [gates(heads + e, e, keep_other) for e in range(early)]
            early_copies[2].wait_recv()
            gf[:, extra] = jnp.dot(perm, g_in[...].astype(bf16), preferred_element_type=f32)
            for e in range(early):
                found, _ = chunks(heads + e, *firsts[e])
                for k, value in enumerate(found):
                    ends_in[e, k] = value

    for copy in summaries:
        copy.wait_recv()

    def entering(place):
        state_in = jnp.zeros((half, 128), f32)
        adj_in = jnp.zeros((half, 128), f32)
        for s in range(count):
            longer = sums[s, :half] * state_in + sums[s, half : 2 * half]
            state_in = jnp.where(s < place, longer, state_in)
            t = count - 1 - s
            longer = sums[t, :half] * adj_in + sums[t, 2 * half :]
            adj_in = jnp.where(t > place, longer, adj_in)
        return state_in, adj_in

    def lanes_of(value, h):
        return jnp.concatenate([value[h * per + l : h * per + l + 1] for l in range(per)], axis=1)

    def second(u, h, enter):
        ch = slice(u * hd, (u + 1) * hd)
        ex_p, ex_s, ex_q, ex_u = ends[u] if u < heads else [ends_in[u - heads, k] for k in range(4)]
        start = ex_s + ex_p * lanes_of(enter[0], h)
        prev = start
        later = ex_u + ex_q * lanes_of(enter[1], h)
        for i in range(0, steps, 2):
            got = []
            for j in (i, i + 1):
                rs = slice(j * SUB, (j + 1) * SUB)
                state = s_s[rs, ch] + p_s[rs, ch] * start
                adj = la_s[rs, ch] + q_s[rs, ch] * later
                dgate = adj * (c1a_s[rs, ch] * prev + c1b_s[rs, ch])
                own = (state, adj * c3_s[rs, ch]) if u < heads else ()
                got.append((dgate, adj * c2_s[rs, ch]) + own)
                prev = state
            both = slice(i * SUB, (i + 2) * SUB)
            pair = [jnp.concatenate(two) for two in zip(*got)]
            dpre[both, u * hm : u * hm + hd] = pair[0].astype(bf16)
            dpre[both, u * hm + hd : (u + 1) * hm] = pair[1].astype(bf16)
            if u < heads:
                outp[both, ch] = pair[2].astype(bf16)
                gxp[both, ch] = pair[3]

    block = ctxs * (hd // count)

    def product(u, to_dp):
        left = xt[pl.ds(pl.multiple_of(u * hd + to_dp * block, block), block), :]
        return jnp.dot(left, dpre[:, u * hm : (u + 1) * hm], preferred_element_type=f32)

    def shard(flips):
        place = 0
        for i, f in enumerate(flips):
            bit = (my_ctx // (1 << i)) % 2
            place = place + (1 << i) * (1 - bit if f else bit)
        return place

    order = orders(bits)
    stage_one = {}
    stage_two = {}

    shards = {flips: shard(flips) for flips in order}
    partners = [lax.rem(my_dp + d, dps) for d in range(dps)]
    for h in range(heads):
        for d in range(1, dps):
            for flips in order:
                k = number(flips)
                stage_one[h, d, k] = describe(
                    gwp.at[h, partners[d], shards[flips]], recv1.at[h, d - 1, k],
                    one_send.at[h, d - 1, k], one_recv.at[h, d - 1, k], {"dp": partners[d]},
                )

    def first_stage(h):
        for d in range(1, dps):
            gwp[h, partners[d]] = product(h, partners[d]).reshape(ctxs, hd // count, hm)
            for flips in order:
                stage_one[h, d, number(flips)].start()

    def mine(h, both=False):
        part = product(h, my_dp)
        if both:
            part = part + product(heads + h, my_dp)
        gwp[h, my_dp] = part.reshape(ctxs, hd // count, hm)

    def slot(step, flips):
        return sum(1 << (bits - 1 - i) for i in range(step)) + number(flips[step + 1 :])

    for h in range(heads):
        for flips in order[:-1]:
            step = flips.index(1)
            bit = (my_ctx // (1 << step)) % 2
            k = slot(step, flips)
            stage_two[h, k] = describe(
                sbuf.at[h, k], recv2.at[h, k], two_send.at[h, k], two_recv.at[h, k],
                {"ctx": my_ctx + (1 << step) * (1 - 2 * bit)},
            )

    def arrived(h, flips):
        for d in range(1, dps):
            stage_one[h, d, number(flips)].wait_recv()
            gwp[h, my_dp, shards[flips]] += recv1[h, d - 1, number(flips)]

    def second_stage(h, flips, lent=None):
        step = flips.index(1) if 1 in flips else bits
        if h >= early or lent is False:
            arrived(h, flips)
        elif lent is None:
            pl.when(keeps)(functools.partial(arrived, h, flips))
        total = gwp[h, my_dp, shards[flips]]
        for i in range(step):
            stage_two[h, slot(i, flips)].wait_recv()
            total = total + recv2[h, slot(i, flips)]
        if step == bits:
            gw_ref[:, h, :] = total
            return
        k = slot(step, flips)
        sbuf[h, k] = total
        stage_two[h, k].start()

    def finish(h):
        ch = slice(h * hd, (h + 1) * hd)
        back = lax.dot_general(
            dpre[:, h * hm : (h + 1) * hm], w_ref[h], (((1,), (1,)), ((), ())),
            preferred_element_type=f32,
        )
        whole = (gxp[:, ch] + back).astype(bf16)
        gx_ref[:, ch] = jnp.dot(unperm, whole, preferred_element_type=f32).astype(bf16)
        out_ref[:, ch] = jnp.dot(unperm, outp[:, ch], preferred_element_type=f32).astype(bf16)

    enter = entering(me)
    for h in range(early, heads):
        second(h, h, enter)
        first_stage(h)
    for h in range(early):
        second(h, h, enter)
    stores = [
        pltpu.make_async_copy(source, target, stored.at[k])
        for k, (source, target) in enumerate(
            ((out_ref, out_hbm), (gx_ref, gx_hbm), (gw_ref, gw_hbm))
        )
    ]
    enter_other = entering((1 - my_dp) * ctxs + my_ctx) if early else None
    near, far = order[: ctxs // 2], order[ctxs // 2 : -1]
    if early:

        @pl.when(lend)
        def _():
            for e in range(early):
                second(heads + e, e, enter_other)
                mine(e, True)
                for flips in near:
                    second_stage(e, flips, True)

        @pl.when(keeps)
        def _():
            for e in range(early):
                first_stage(e)
                mine(e)

    for h in range(early, heads):
        mine(h)
    finish(0)
    for h in range(early, heads):
        for flips in near:
            second_stage(h, flips)
    if early:

        @pl.when(lend)
        def _():
            for e in range(early):
                for flips in far:
                    second_stage(e, flips, True)

    for h in range(1, heads):
        finish(h)
    stores[0].start()
    stores[1].start()
    if early:

        @pl.when(keeps)
        def _():
            for e in range(early):
                for flips in near:
                    second_stage(e, flips, False)

    for h in range(early, heads):
        for flips in far:
            second_stage(h, flips)
    if early:

        @pl.when(keeps)
        def _():
            for e in range(early):
                for flips in far:
                    second_stage(e, flips, False)

    for h in range(early, heads):
        second_stage(h, order[-1])
    for h in range(early):
        second_stage(h, order[-1])
    stores[2].start()
    for store in stores:
        store.wait()
    for copy in sends + list(stage_two.values()):
        copy.wait_send()
    for (h, _, _), copy in stage_one.items():
        if h >= early:
            copy.wait_send()
    if early:

        @pl.when(lend)
        def _():
            for copy in early_copies:
                copy.wait_send()

        @pl.when(keeps)
        def _():
            for (h, _, _), copy in stage_one.items():
                if h < early:
                    copy.wait_send()


def write_out(out_in, gx_in, gw_in, out_hbm, gx_hbm, gw_hbm, out_ref, gx_ref, gw_ref, came, done):
    ins = [
        pltpu.make_async_copy(source, target, came.at[k])
        for k, (source, target) in enumerate(((out_in, out_ref), (gx_in, gx_ref), (gw_in, gw_ref)))
    ]
    outs = [
        pltpu.make_async_copy(source, target, done.at[k])
        for k, (source, target) in enumerate(
            ((out_ref, out_hbm), (gx_ref, gx_hbm), (gw_ref, gw_hbm))
        )
    ]
    for copy in ins:
        copy.start()
    for copy, after in zip(ins, outs):
        copy.wait()
        after.start()
    for copy in outs:
        copy.wait()


def per_device(dps, ctxs, inputs, doc_start, gate_weight, gate_bias, decay_rate, cotangent):
    batch_rows, rows, width = inputs.shape
    hd, heads, hm = gate_weight.shape
    count = dps * ctxs
    early = 1 if dps == 2 and heads > 1 else 0
    lent = max(early, 1) * hd
    f32, bf16 = jnp.float32, jnp.bfloat16
    part = hd // count
    full = pltpu.VMEM((rows, width + lent), f32)
    half = pltpu.VMEM((rows, width), bf16)
    sent = pltpu.VMEM((rows, lent), f32)
    lane_rows = 3 * (width // 128)
    hbm = pl.BlockSpec(memory_space=pltpu.HBM)
    params = dict(vmem_limit_bytes=60 * 1024 * 1024)
    shapes = (
        jax.ShapeDtypeStruct((rows, width), bf16),
        jax.ShapeDtypeStruct((rows, width), bf16),
        jax.ShapeDtypeStruct((part, heads, hm), f32),
    )
    held = pl.pallas_call(
        functools.partial(kernel, dps, ctxs, early),
        out_shape=shapes,
        in_specs=[hbm] * 6,
        out_specs=(hbm,) * 3,
        scratch_shapes=[
            half, pltpu.VMEM((1, rows), jnp.int32), pltpu.VMEM((hd, heads, hm), bf16),
            pltpu.VMEM((heads, hm), f32), pltpu.VMEM((1, width), f32), half,
            pltpu.VMEM((heads, hd, hm), bf16), pltpu.SemaphoreType.DMA((6,)),
            pltpu.VMEM((heads, part, hm), f32), half, half, pltpu.VMEM((part, heads, hm), f32),
            pltpu.SemaphoreType.DMA((3,)),
            sent, sent, pltpu.VMEM((SUB, rows), f32), sent, sent, pltpu.VMEM((SUB, rows), f32),
            pltpu.VMEM((max(early, 1), 4, SUB, hd), f32),
            full, pltpu.VMEM((rows, width + lent), bf16), pltpu.VMEM((width + lent, rows), bf16),
            full, pltpu.VMEM((rows, (heads + max(early, 1)) * hm), f32),
            full, full, full, full, full, full, full, full, full,
            half, pltpu.VMEM((rows, (heads + max(early, 1)) * hm), bf16),
            pltpu.VMEM((rows, width), f32),
            pltpu.VMEM((count, lane_rows, 128), f32),
            pltpu.VMEM((heads, dps, ctxs, part, hm), f32),
            pltpu.VMEM((heads, dps - 1, ctxs, part, hm), f32),
            pltpu.VMEM((heads, ctxs - 1, part, hm), f32),
            pltpu.VMEM((heads, ctxs - 1, part, hm), f32),
            pltpu.SemaphoreType.DMA((3,)),
            pltpu.SemaphoreType.DMA((3,)),
            pltpu.SemaphoreType.DMA((count - 1,)),
            pltpu.SemaphoreType.DMA((count - 1,)),
            pltpu.SemaphoreType.DMA((heads, dps - 1, ctxs)),
            pltpu.SemaphoreType.DMA((heads, dps - 1, ctxs)),
            pltpu.SemaphoreType.DMA((heads, ctxs - 1)),
            pltpu.SemaphoreType.DMA((heads, ctxs - 1)),
        ],
        compiler_params=pltpu.CompilerParams(collective_id=0, has_side_effects=True, **params),
    )(
        inputs.reshape(rows, width), doc_start.reshape(1, rows), gate_weight, gate_bias,
        decay_rate.reshape(1, width), cotangent.reshape(rows, width),
    )
    out, gx, gw = pl.pallas_call(
        write_out,
        out_shape=shapes,
        in_specs=[hbm] * 3,
        out_specs=(hbm,) * 3,
        scratch_shapes=[
            half, half, pltpu.VMEM((part, heads, hm), f32),
            pltpu.SemaphoreType.DMA((3,)), pltpu.SemaphoreType.DMA((3,)),
        ],
        compiler_params=pltpu.CompilerParams(**params),
    )(*held)
    return (out.reshape(batch_rows, rows, width), gx.reshape(batch_rows, rows, width), gw)


def solution(mesh):
    in_specs = (
        P(None, ("dp", "ctx"), "mp"),
        P(None, ("dp", "ctx")),
        P(None, "mp", None),
        P("mp", None),
        P("mp"),
        P(None, ("dp", "ctx"), "mp"),
    )
    out_specs = (
        P(None, ("dp", "ctx"), "mp"),
        P(None, ("dp", "ctx"), "mp"),
        P(("dp", "ctx"), "mp", None),
    )
    return jax.shard_map(
        functools.partial(per_device, mesh.shape["dp"], mesh.shape["ctx"]),
        mesh=mesh, in_specs=in_specs, out_specs=out_specs, check_vma=False,
    )
```

```python
import functools

import jax
import jax.numpy as jnp
from jax import lax
from jax.experimental import pallas as pl
from jax.experimental.pallas import tpu as pltpu
from jax.sharding import PartitionSpec as P

MESH = pl.DeviceIdType.MESH
SUB = 8


def orders(bits):
    return [()] if bits == 0 else [(f,) + o for f in (1, 0) for o in orders(bits - 1)]


def number(flips):
    return sum(f << i for i, f in enumerate(flips))


def kernel(
    dps, ctxs, early, x_hbm, doc_hbm, w_hbm, bias_hbm, rate_hbm, g_hbm, out_hbm, gx_hbm, gw_hbm,
    x_ref, doc_ref, w_pairs, bias_ref, rate_ref, g_ref, w_ref, loaded, gw_sum,
    out_ref, gx_ref, gw_ref, stored,
    x_out, g_out, doc_out, x_in, g_in, doc_in,
    xf, xb, xt, gf, pre, carry_s, s_s, p_s, la_s, q_s, c1a_s, c1b_s, c2_s, c3_s, outp, dpre,
    gxp, sums, gwp, recv1, sbuf, recv2,
    early_send, early_recv, sum_send, sum_recv, one_send, one_recv, two_send, two_recv,
):
    rows, width = x_ref.shape
    heads, hd, hm = w_ref.shape
    loads = [
        pltpu.make_async_copy(source, target, loaded.at[k])
        for k, (source, target) in enumerate((
            (x_hbm, x_ref), (doc_hbm, doc_ref), (g_hbm, g_ref), (w_hbm, w_pairs),
            (bias_hbm, bias_ref), (rate_hbm, rate_ref),
        ))
    ]
    for load in loads:
        load.start()
    count = dps * ctxs
    steps = rows // SUB
    bits = ctxs.bit_length() - 1
    my_dp, my_ctx = lax.axis_index("dp"), lax.axis_index("ctx")
    me = my_dp * ctxs + my_ctx
    f32, bf16 = jnp.float32, jnp.bfloat16
    sends = []

    barrier = pltpu.get_barrier_semaphore()
    for d in range(1, count):
        to = lax.rem(me + d, count)
        pl.semaphore_signal(
            barrier, inc=1, device_id={"dp": to // ctxs, "ctx": lax.rem(to, ctxs)},
            device_id_type=MESH,
        )

    def send(source, target, send_sem, recv_sem, device):
        copy = pltpu.make_async_remote_copy(
            src_ref=source, dst_ref=target, send_sem=send_sem, recv_sem=recv_sem,
            device_id=device, device_id_type=MESH,
        )
        copy.start()
        sends.append(copy)
        return copy

    row = lax.broadcasted_iota(jnp.int32, (rows, rows), 0)
    col = lax.broadcasted_iota(jnp.int32, (rows, rows), 1)
    low = SUB.bit_length() - 1
    here = (row & (SUB - 1)) * steps + (row >> low) == col
    back_here = (col & (SUB - 1)) * steps + (col >> low) == row
    perm = jnp.where(here, 1.0, 0.0).astype(bf16)
    unperm = jnp.where(back_here, 1.0, 0.0).astype(bf16)
    wide_row = lax.broadcasted_iota(jnp.int32, (hd, heads * hd), 0)
    wide_col = lax.broadcasted_iota(jnp.int32, (hd, heads * hd), 1)
    spread = [
        jnp.where(wide_row * heads + h == wide_col, 1.0, 0.0).astype(bf16) for h in range(heads)
    ]
    chunk = lax.broadcasted_iota(jnp.int32, (SUB, hd), 0)

    for load in loads[:3]:
        load.wait()
    doc_float = doc_ref[...].astype(f32)
    if early:
        x_out[...] = x_ref[:, : early * hd].astype(f32)
        g_out[...] = g_ref[:, : early * hd].astype(f32)
        doc_out[...] = jnp.broadcast_to(doc_float, doc_out.shape)
    pl.semaphore_wait(barrier, count - 1)
    early_copies = []
    if early:
        other = {"dp": 1 - my_dp}
        for k, (source, target) in enumerate(((doc_out, doc_in), (x_out, x_in))):
            early_copies.append(
                send(source, target, early_send.at[k], early_recv.at[k], other)
            )
        first = lax.rem(lax.axis_index("mp"), 2) == 0
        early_copies.append(pltpu.make_async_remote_copy(
            src_ref=g_out, dst_ref=g_in, send_sem=early_send.at[2], recv_sem=early_recv.at[2],
            device_id=other, device_id_type=MESH,
        ))
        sends.append(early_copies[2])
        pl.when(first)(early_copies[2].start)

    def keep_of(doc):
        return 1.0 - jnp.sum(jnp.where(here, doc, 0.0), axis=1, keepdims=True)

    def project(u, h, w_all):
        ch = slice(u * hd, (u + 1) * hd)
        spread_x = jnp.dot(xb[:, ch], spread[h], preferred_element_type=f32).astype(bf16)
        pre[:, u * hm : (u + 1) * hm] = (
            jnp.dot(spread_x, w_all, preferred_element_type=f32) + bias_ref[h : h + 1, :]
        )

    def gates(u, h, keep_col):
        ch = slice(u * hd, (u + 1) * hd)
        rate8 = -8.0 * rate_ref[:, h * hd : (h + 1) * hd]
        state = prod = None
        for i in range(steps):
            rs = slice(i * SUB, (i + 1) * SUB)
            x = xf[rs, ch]
            keep = jnp.broadcast_to(keep_col[rs], (SUB, hd))
            kept = keep > 0.5
            rgate = 0.5 * jnp.tanh(0.5 * pre[rs, u * hm : u * hm + hd]) + 0.5
            igate = 0.5 * jnp.tanh(0.5 * pre[rs, u * hm + hd : (u + 1) * hm]) + 0.5
            decay = jnp.exp(rate8 * rgate)
            square = decay * decay
            inside = 1.0 - square + 0.01
            inverse = lax.rsqrt(inside)
            carry = decay * keep
            scale = jnp.where(kept, inside * inverse, 1.0)
            gated = igate * x
            drive = scale * gated
            c1 = rate8 * rgate * (1.0 - rgate)
            carry_s[rs, ch] = carry
            c1a_s[rs, ch] = carry * c1
            c1b_s[rs, ch] = gated * jnp.where(kept, -square * inverse, 0.0) * c1
            c2_s[rs, ch] = drive * (1.0 - igate)
            if u < heads:
                c3_s[rs, ch] = scale * igate
            if i == 0:
                state, prod = drive, carry
            else:
                state, prod = carry * state + drive, carry * prod
            s_s[rs, ch] = state
            p_s[rs, ch] = prod
        return state, prod

    def chunks(u, state, prod):
        ch = slice(u * hd, (u + 1) * hd)
        adj = gf[(steps - 1) * SUB :, ch]
        tail = jnp.ones((SUB, hd), f32)
        la_s[(steps - 1) * SUB :, ch] = adj
        q_s[(steps - 1) * SUB :, ch] = tail
        for i in range(steps - 2, -1, -1):
            rs = slice(i * SUB, (i + 1) * SUB)
            after = carry_s[(i + 1) * SUB : (i + 2) * SUB, ch]
            adj = gf[rs, ch] + after * adj
            tail = after * tail
            la_s[rs, ch] = adj
            q_s[rs, ch] = tail
        fs, fp = state, prod
        bu, bp = carry_s[:SUB, ch] * adj, prod
        s = 1
        while s < SUB:
            ok = chunk >= s
            rolled_p, rolled_s = pltpu.roll(fp, s, 0), pltpu.roll(fs, s, 0)
            fs = jnp.where(ok, fp * rolled_s + fs, fs)
            fp = jnp.where(ok, fp * rolled_p, fp)
            ok = chunk < SUB - s
            rolled_p, rolled_s = pltpu.roll(bp, SUB - s, 0), pltpu.roll(bu, SUB - s, 0)
            bu = jnp.where(ok, bp * rolled_s + bu, bu)
            bp = jnp.where(ok, bp * rolled_p, bp)
            s *= 2
        ends = (
            jnp.where(chunk >= 1, pltpu.roll(fp, 1, 0), 1.0),
            jnp.where(chunk >= 1, pltpu.roll(fs, 1, 0), 0.0),
            jnp.where(chunk < SUB - 1, pltpu.roll(bp, SUB - 1, 0), 1.0),
            jnp.where(chunk < SUB - 1, pltpu.roll(bu, SUB - 1, 0), 0.0),
        )
        return ends, (fp[SUB - 1 :], fs[SUB - 1 :], bu[:1])

    per = hd // 128
    half = width // 128
    keep_col = keep_of(doc_float)
    xf[:, :width] = jnp.dot(perm, x_ref[...], preferred_element_type=f32)
    xb[:, :width] = xf[:, :width].astype(bf16)
    gf[:, :width] = jnp.dot(perm, g_ref[...], preferred_element_type=f32)
    for load in loads[3:]:
        load.wait()
    w_all = w_pairs[...].reshape(hd * heads, hm)
    ends = {}
    for h in range(heads):
        project(h, h, w_all)
    for h in range(heads):
        ends[h], whole = chunks(h, *gates(h, h, keep_col))
        for k, value in enumerate(whole):
            for l in range(per):
                at = k * half + h * per + l
                sums[me, at : at + 1] = value[:, l * 128 : (l + 1) * 128]

    summaries = []
    for d in range(1, count):
        to = lax.rem(me + d, count)
        summaries.append(send(
            sums.at[me], sums.at[me], sum_send.at[d - 1], sum_recv.at[d - 1],
            {"dp": to // ctxs, "ctx": lax.rem(to, ctxs)},
        ))

    if early:
        pl.when(jnp.logical_not(first))(early_copies[2].start)

    for h in range(heads):
        xt[h * hd : (h + 1) * hd, :] = jnp.transpose(xf[:, h * hd : (h + 1) * hd]).astype(bf16)

    for h in range(heads):
        w_ref[h] = jnp.dot(spread[h], w_all, preferred_element_type=f32).astype(bf16)
    if early:
        extra = slice(width, width + early * hd)
        early_copies[0].wait_recv()
        early_copies[1].wait_recv()
        keep_other = keep_of(doc_in[:1])
        xf[:, extra] = jnp.dot(perm, x_in[...].astype(bf16), preferred_element_type=f32)
        xb[:, extra] = xf[:, extra].astype(bf16)
        xt[extra, :] = jnp.transpose(xf[:, extra]).astype(bf16)
        for e in range(early):
            project(heads + e, e, w_all)
        firsts = [gates(heads + e, e, keep_other) for e in range(early)]
        early_copies[2].wait_recv()
        gf[:, extra] = jnp.dot(perm, g_in[...].astype(bf16), preferred_element_type=f32)
        for e in range(early):
            ends[heads + e], _ = chunks(heads + e, *firsts[e])

    for copy in summaries:
        copy.wait_recv()

    def entering(place):
        state_in = jnp.zeros((half, 128), f32)
        adj_in = jnp.zeros((half, 128), f32)
        for s in range(count):
            longer = sums[s, :half] * state_in + sums[s, half : 2 * half]
            state_in = jnp.where(s < place, longer, state_in)
            t = count - 1 - s
            longer = sums[t, :half] * adj_in + sums[t, 2 * half :]
            adj_in = jnp.where(t > place, longer, adj_in)
        return state_in, adj_in

    def lanes_of(value, h):
        return jnp.concatenate([value[h * per + l : h * per + l + 1] for l in range(per)], axis=1)

    def second(u, h, enter):
        ch = slice(u * hd, (u + 1) * hd)
        ex_p, ex_s, ex_q, ex_u = ends[u]
        start = ex_s + ex_p * lanes_of(enter[0], h)
        prev = start
        later = ex_u + ex_q * lanes_of(enter[1], h)
        for i in range(0, steps, 2):
            got = []
            for j in (i, i + 1):
                rs = slice(j * SUB, (j + 1) * SUB)
                state = s_s[rs, ch] + p_s[rs, ch] * start
                adj = la_s[rs, ch] + q_s[rs, ch] * later
                dgate = adj * (c1a_s[rs, ch] * prev + c1b_s[rs, ch])
                own = (state, adj * c3_s[rs, ch]) if u < heads else ()
                got.append((dgate, adj * c2_s[rs, ch]) + own)
                prev = state
            both = slice(i * SUB, (i + 2) * SUB)
            pair = [jnp.concatenate(two) for two in zip(*got)]
            dpre[both, u * hm : u * hm + hd] = pair[0].astype(bf16)
            dpre[both, u * hm + hd : (u + 1) * hm] = pair[1].astype(bf16)
            if u < heads:
                outp[both, ch] = pair[2].astype(bf16)
                gxp[both, ch] = pair[3]

    block = ctxs * (hd // count)

    def product(u, to_dp):
        left = xt[pl.ds(pl.multiple_of(u * hd + to_dp * block, block), block), :]
        return jnp.dot(left, dpre[:, u * hm : (u + 1) * hm], preferred_element_type=f32)

    def shard(flips):
        place = 0
        for i, f in enumerate(flips):
            bit = (my_ctx // (1 << i)) % 2
            place = place + (1 << i) * (1 - bit if f else bit)
        return place

    order = orders(bits)
    stage_one = {}
    stage_two = {}

    def first_stage(h):
        for d in range(1, dps):
            to_dp = lax.rem(my_dp + d, dps)
            gwp[h, to_dp] = product(h, to_dp).reshape(ctxs, hd // count, hm)
            for flips in order:
                k = number(flips)
                stage_one[h, d, k] = send(
                    gwp.at[h, to_dp, shard(flips)], recv1.at[h, d - 1, k],
                    one_send.at[h, d - 1, k], one_recv.at[h, d - 1, k], {"dp": to_dp},
                )

    def mine(h):
        part = product(h, my_dp)
        if h < early:
            part = part + product(heads + h, my_dp)
        gwp[h, my_dp] = part.reshape(ctxs, hd // count, hm)

    def slot(step, flips):
        return sum(1 << (bits - 1 - i) for i in range(step)) + number(flips[step + 1 :])

    def second_stage(h, flips):
        step = flips.index(1) if 1 in flips else bits
        total = gwp[h, my_dp, shard(flips)]
        if h >= early:
            for d in range(1, dps):
                stage_one[h, d, number(flips)].wait_recv()
                total = total + recv1[h, d - 1, number(flips)]
        for i in range(step):
            stage_two[h, slot(i, flips)].wait_recv()
            total = total + recv2[h, slot(i, flips)]
        if step == bits:
            gw_ref[:, h, :] = total
            return
        k = slot(step, flips)
        sbuf[h, k] = total
        bit = (my_ctx // (1 << step)) % 2
        stage_two[h, k] = send(
            sbuf.at[h, k], recv2.at[h, k], two_send.at[h, k], two_recv.at[h, k],
            {"ctx": my_ctx + (1 << step) * (1 - 2 * bit)},
        )

    def finish(h):
        ch = slice(h * hd, (h + 1) * hd)
        back = lax.dot_general(
            dpre[:, h * hm : (h + 1) * hm], w_ref[h], (((1,), (1,)), ((), ())),
            preferred_element_type=f32,
        )
        whole = (gxp[:, ch] + back).astype(bf16)
        gx_ref[:, ch] = jnp.dot(unperm, whole, preferred_element_type=f32).astype(bf16)
        out_ref[:, ch] = jnp.dot(unperm, outp[:, ch], preferred_element_type=f32).astype(bf16)

    enter = entering(me)
    for h in range(early, heads):
        second(h, h, enter)
        first_stage(h)
    for h in range(early):
        second(h, h, enter)
    stores = [
        pltpu.make_async_copy(source, target, stored.at[k])
        for k, (source, target) in enumerate(
            ((out_ref, out_hbm), (gx_ref, gx_hbm), (gw_ref, gw_hbm))
        )
    ]
    enter_other = entering((1 - my_dp) * ctxs + my_ctx) if early else None
    for e in range(early):
        second(heads + e, e, enter_other)
        mine(e)
        for flips in order[: ctxs // 2]:
            second_stage(e, flips)
    for h in range(early, heads):
        mine(h)
    finish(0)
    for h in range(early, heads):
        for flips in order[: ctxs // 2]:
            second_stage(h, flips)
    for h in range(early):
        for flips in order[ctxs // 2 : -1]:
            second_stage(h, flips)
    for h in range(1, heads):
        finish(h)
    stores[0].start()
    stores[1].start()
    for h in range(early, heads):
        for flips in order[ctxs // 2 : -1]:
            second_stage(h, flips)
    for h in range(heads):
        second_stage(h, order[-1])
    stores[2].start()
    for store in stores:
        store.wait()
    for copy in sends:
        copy.wait_send()


def write_out(out_in, gx_in, gw_in, out_hbm, gx_hbm, gw_hbm, out_ref, gx_ref, gw_ref, came, done):
    ins = [
        pltpu.make_async_copy(source, target, came.at[k])
        for k, (source, target) in enumerate(((out_in, out_ref), (gx_in, gx_ref), (gw_in, gw_ref)))
    ]
    outs = [
        pltpu.make_async_copy(source, target, done.at[k])
        for k, (source, target) in enumerate(
            ((out_ref, out_hbm), (gx_ref, gx_hbm), (gw_ref, gw_hbm))
        )
    ]
    for copy in ins:
        copy.start()
    for copy, after in zip(ins, outs):
        copy.wait()
        after.start()
    for copy in outs:
        copy.wait()


def per_device(dps, ctxs, inputs, doc_start, gate_weight, gate_bias, decay_rate, cotangent):
    batch_rows, rows, width = inputs.shape
    hd, heads, hm = gate_weight.shape
    count = dps * ctxs
    early = 1 if dps == 2 and heads > 1 else 0
    lent = max(early, 1) * hd
    f32, bf16 = jnp.float32, jnp.bfloat16
    part = hd // count
    full = pltpu.VMEM((rows, width + lent), f32)
    half = pltpu.VMEM((rows, width), bf16)
    sent = pltpu.VMEM((rows, lent), f32)
    lane_rows = 3 * (width // 128)
    hbm = pl.BlockSpec(memory_space=pltpu.HBM)
    params = dict(vmem_limit_bytes=60 * 1024 * 1024)
    shapes = (
        jax.ShapeDtypeStruct((rows, width), bf16),
        jax.ShapeDtypeStruct((rows, width), bf16),
        jax.ShapeDtypeStruct((part, heads, hm), f32),
    )
    held = pl.pallas_call(
        functools.partial(kernel, dps, ctxs, early),
        out_shape=shapes,
        in_specs=[hbm] * 6,
        out_specs=(hbm,) * 3,
        scratch_shapes=[
            half, pltpu.VMEM((1, rows), jnp.int32), pltpu.VMEM((hd, heads, hm), bf16),
            pltpu.VMEM((heads, hm), f32), pltpu.VMEM((1, width), f32), half,
            pltpu.VMEM((heads, hd, hm), bf16), pltpu.SemaphoreType.DMA((6,)),
            pltpu.VMEM((heads, part, hm), f32), half, half, pltpu.VMEM((part, heads, hm), f32),
            pltpu.SemaphoreType.DMA((3,)),
            sent, sent, pltpu.VMEM((SUB, rows), f32), sent, sent, pltpu.VMEM((SUB, rows), f32),
            full, pltpu.VMEM((rows, width + lent), bf16), pltpu.VMEM((width + lent, rows), bf16),
            full, pltpu.VMEM((rows, (heads + max(early, 1)) * hm), f32),
            full, full, full, full, full, full, full, full, full,
            half, pltpu.VMEM((rows, (heads + max(early, 1)) * hm), bf16),
            pltpu.VMEM((rows, width), f32),
            pltpu.VMEM((count, lane_rows, 128), f32),
            pltpu.VMEM((heads, dps, ctxs, part, hm), f32),
            pltpu.VMEM((heads, dps - 1, ctxs, part, hm), f32),
            pltpu.VMEM((heads, ctxs - 1, part, hm), f32),
            pltpu.VMEM((heads, ctxs - 1, part, hm), f32),
            pltpu.SemaphoreType.DMA((3,)),
            pltpu.SemaphoreType.DMA((3,)),
            pltpu.SemaphoreType.DMA((count - 1,)),
            pltpu.SemaphoreType.DMA((count - 1,)),
            pltpu.SemaphoreType.DMA((heads, dps - 1, ctxs)),
            pltpu.SemaphoreType.DMA((heads, dps - 1, ctxs)),
            pltpu.SemaphoreType.DMA((heads, ctxs - 1)),
            pltpu.SemaphoreType.DMA((heads, ctxs - 1)),
        ],
        compiler_params=pltpu.CompilerParams(collective_id=0, has_side_effects=True, **params),
    )(
        inputs.reshape(rows, width), doc_start.reshape(1, rows), gate_weight, gate_bias,
        decay_rate.reshape(1, width), cotangent.reshape(rows, width),
    )
    out, gx, gw = pl.pallas_call(
        write_out,
        out_shape=shapes,
        in_specs=[hbm] * 3,
        out_specs=(hbm,) * 3,
        scratch_shapes=[
            half, half, pltpu.VMEM((part, heads, hm), f32),
            pltpu.SemaphoreType.DMA((3,)), pltpu.SemaphoreType.DMA((3,)),
        ],
        compiler_params=pltpu.CompilerParams(**params),
    )(*held)
    return (out.reshape(batch_rows, rows, width), gx.reshape(batch_rows, rows, width), gw)


def solution(mesh):
    in_specs = (
        P(None, ("dp", "ctx"), "mp"),
        P(None, ("dp", "ctx")),
        P(None, "mp", None),
        P("mp", None),
        P("mp"),
        P(None, ("dp", "ctx"), "mp"),
    )
    out_specs = (
        P(None, ("dp", "ctx"), "mp"),
        P(None, ("dp", "ctx"), "mp"),
        P(("dp", "ctx"), "mp", None),
    )
    return jax.shard_map(
        functools.partial(per_device, mesh.shape["dp"], mesh.shape["ctx"]),
        mesh=mesh, in_specs=in_specs, out_specs=out_specs, check_vma=False,
    )
```

```python
import functools

import jax
import jax.numpy as jnp
from jax import lax
from jax.experimental import pallas as pl
from jax.experimental.pallas import tpu as pltpu
from jax.sharding import PartitionSpec as P

MESH = pl.DeviceIdType.MESH
SUB = 8


def orders(bits):
    return [()] if bits == 0 else [(f,) + o for f in (1, 0) for o in orders(bits - 1)]


def number(flips):
    return sum(f << i for i, f in enumerate(flips))


def kernel(
    dps, ctxs, early, x_hbm, doc_hbm, w_hbm, bias_hbm, rate_hbm, g_hbm, out_hbm, gx_hbm, gw_hbm,
    x_ref, doc_ref, w_pairs, bias_ref, rate_ref, g_ref, w_ref, loaded, gw_sum,
    out_ref, gx_ref, gw_ref, stored,
    x_out, g_out, doc_out, x_in, g_in, doc_in,
    xf, xb, xt, gf, pre, carry_s, s_s, p_s, la_s, q_s, c1a_s, c1b_s, c2_s, c3_s, outp, dpre,
    gxp, sums, gwp, recv1, sbuf, recv2,
    early_send, early_recv, sum_send, sum_recv, one_send, one_recv, two_send, two_recv,
):
    rows, width = x_ref.shape
    heads, hd, hm = w_ref.shape
    loads = [
        pltpu.make_async_copy(source, target, loaded.at[k])
        for k, (source, target) in enumerate((
            (x_hbm, x_ref), (doc_hbm, doc_ref), (g_hbm, g_ref), (w_hbm, w_pairs),
            (bias_hbm, bias_ref), (rate_hbm, rate_ref),
        ))
    ]
    for load in loads:
        load.start()
    count = dps * ctxs
    steps = rows // SUB
    bits = ctxs.bit_length() - 1
    my_dp, my_ctx = lax.axis_index("dp"), lax.axis_index("ctx")
    me = my_dp * ctxs + my_ctx
    f32, bf16 = jnp.float32, jnp.bfloat16
    sends = []

    barrier = pltpu.get_barrier_semaphore()
    for d in range(1, count):
        to = lax.rem(me + d, count)
        pl.semaphore_signal(
            barrier, inc=1, device_id={"dp": to // ctxs, "ctx": lax.rem(to, ctxs)},
            device_id_type=MESH,
        )

    def send(source, target, send_sem, recv_sem, device):
        copy = pltpu.make_async_remote_copy(
            src_ref=source, dst_ref=target, send_sem=send_sem, recv_sem=recv_sem,
            device_id=device, device_id_type=MESH,
        )
        copy.start()
        sends.append(copy)
        return copy

    row = lax.broadcasted_iota(jnp.int32, (rows, rows), 0)
    col = lax.broadcasted_iota(jnp.int32, (rows, rows), 1)
    low = SUB.bit_length() - 1
    here = (row & (SUB - 1)) * steps + (row >> low) == col
    back_here = (col & (SUB - 1)) * steps + (col >> low) == row
    perm = jnp.where(here, 1.0, 0.0).astype(bf16)
    unperm = jnp.where(back_here, 1.0, 0.0).astype(bf16)
    wide_row = lax.broadcasted_iota(jnp.int32, (hd, heads * hd), 0)
    wide_col = lax.broadcasted_iota(jnp.int32, (hd, heads * hd), 1)
    spread = [
        jnp.where(wide_row * heads + h == wide_col, 1.0, 0.0).astype(bf16) for h in range(heads)
    ]
    chunk = lax.broadcasted_iota(jnp.int32, (SUB, hd), 0)

    for load in loads[:3]:
        load.wait()
    doc_float = doc_ref[...].astype(f32)
    if early:
        x_out[...] = x_ref[:, : early * hd].astype(f32)
        g_out[...] = g_ref[:, : early * hd].astype(f32)
        doc_out[...] = jnp.broadcast_to(doc_float, doc_out.shape)
    pl.semaphore_wait(barrier, count - 1)
    early_copies = []
    if early:
        other = {"dp": 1 - my_dp}
        for k, (source, target) in enumerate(((doc_out, doc_in), (x_out, x_in), (g_out, g_in))):
            early_copies.append(
                send(source, target, early_send.at[k], early_recv.at[k], other)
            )

    def keep_of(doc):
        return 1.0 - jnp.sum(jnp.where(here, doc, 0.0), axis=1, keepdims=True)

    def project(u, h, w_all):
        ch = slice(u * hd, (u + 1) * hd)
        spread_x = jnp.dot(xb[:, ch], spread[h], preferred_element_type=f32).astype(bf16)
        pre[:, u * hm : (u + 1) * hm] = (
            jnp.dot(spread_x, w_all, preferred_element_type=f32) + bias_ref[h : h + 1, :]
        )

    def gates(u, h, keep_col):
        ch = slice(u * hd, (u + 1) * hd)
        rate8 = -8.0 * rate_ref[:, h * hd : (h + 1) * hd]
        state = prod = None
        for i in range(steps):
            rs = slice(i * SUB, (i + 1) * SUB)
            x = xf[rs, ch]
            keep = jnp.broadcast_to(keep_col[rs], (SUB, hd))
            kept = keep > 0.5
            rgate = 0.5 * jnp.tanh(0.5 * pre[rs, u * hm : u * hm + hd]) + 0.5
            igate = 0.5 * jnp.tanh(0.5 * pre[rs, u * hm + hd : (u + 1) * hm]) + 0.5
            decay = jnp.exp(rate8 * rgate)
            square = decay * decay
            inside = 1.0 - square + 0.01
            inverse = lax.rsqrt(inside)
            carry = decay * keep
            scale = jnp.where(kept, inside * inverse, 1.0)
            gated = igate * x
            drive = scale * gated
            c1 = rate8 * rgate * (1.0 - rgate)
            carry_s[rs, ch] = carry
            c1a_s[rs, ch] = carry * c1
            c1b_s[rs, ch] = gated * jnp.where(kept, -square * inverse, 0.0) * c1
            c2_s[rs, ch] = drive * (1.0 - igate)
            if u < heads:
                c3_s[rs, ch] = scale * igate
            if i == 0:
                state, prod = drive, carry
            else:
                state, prod = carry * state + drive, carry * prod
            s_s[rs, ch] = state
            p_s[rs, ch] = prod
        return state, prod

    def chunks(u, state, prod):
        ch = slice(u * hd, (u + 1) * hd)
        adj = gf[(steps - 1) * SUB :, ch]
        tail = jnp.ones((SUB, hd), f32)
        la_s[(steps - 1) * SUB :, ch] = adj
        q_s[(steps - 1) * SUB :, ch] = tail
        for i in range(steps - 2, -1, -1):
            rs = slice(i * SUB, (i + 1) * SUB)
            after = carry_s[(i + 1) * SUB : (i + 2) * SUB, ch]
            adj = gf[rs, ch] + after * adj
            tail = after * tail
            la_s[rs, ch] = adj
            q_s[rs, ch] = tail
        fs, fp = state, prod
        bu, bp = carry_s[:SUB, ch] * adj, prod
        s = 1
        while s < SUB:
            ok = chunk >= s
            rolled_p, rolled_s = pltpu.roll(fp, s, 0), pltpu.roll(fs, s, 0)
            fs = jnp.where(ok, fp * rolled_s + fs, fs)
            fp = jnp.where(ok, fp * rolled_p, fp)
            ok = chunk < SUB - s
            rolled_p, rolled_s = pltpu.roll(bp, SUB - s, 0), pltpu.roll(bu, SUB - s, 0)
            bu = jnp.where(ok, bp * rolled_s + bu, bu)
            bp = jnp.where(ok, bp * rolled_p, bp)
            s *= 2
        ends = (
            jnp.where(chunk >= 1, pltpu.roll(fp, 1, 0), 1.0),
            jnp.where(chunk >= 1, pltpu.roll(fs, 1, 0), 0.0),
            jnp.where(chunk < SUB - 1, pltpu.roll(bp, SUB - 1, 0), 1.0),
            jnp.where(chunk < SUB - 1, pltpu.roll(bu, SUB - 1, 0), 0.0),
        )
        return ends, (fp[SUB - 1 :], fs[SUB - 1 :], bu[:1])

    per = hd // 128
    half = width // 128
    keep_col = keep_of(doc_float)
    xf[:, :width] = jnp.dot(perm, x_ref[...], preferred_element_type=f32)
    xb[:, :width] = xf[:, :width].astype(bf16)
    gf[:, :width] = jnp.dot(perm, g_ref[...], preferred_element_type=f32)
    for load in loads[3:]:
        load.wait()
    w_all = w_pairs[...].reshape(hd * heads, hm)
    ends = {}
    for h in range(heads):
        project(h, h, w_all)
    for h in range(heads):
        ends[h], whole = chunks(h, *gates(h, h, keep_col))
        for k, value in enumerate(whole):
            for l in range(per):
                at = k * half + h * per + l
                sums[me, at : at + 1] = value[:, l * 128 : (l + 1) * 128]

    summaries = []
    for d in range(1, count):
        to = lax.rem(me + d, count)
        summaries.append(send(
            sums.at[me], sums.at[me], sum_send.at[d - 1], sum_recv.at[d - 1],
            {"dp": to // ctxs, "ctx": lax.rem(to, ctxs)},
        ))

    for h in range(heads):
        xt[h * hd : (h + 1) * hd, :] = jnp.transpose(xf[:, h * hd : (h + 1) * hd]).astype(bf16)

    for h in range(heads):
        w_ref[h] = jnp.dot(spread[h], w_all, preferred_element_type=f32).astype(bf16)
    if early:
        extra = slice(width, width + early * hd)
        early_copies[0].wait_recv()
        early_copies[1].wait_recv()
        keep_other = keep_of(doc_in[:1])
        xf[:, extra] = jnp.dot(perm, x_in[...].astype(bf16), preferred_element_type=f32)
        xb[:, extra] = xf[:, extra].astype(bf16)
        xt[extra, :] = jnp.transpose(xf[:, extra]).astype(bf16)
        for e in range(early):
            project(heads + e, e, w_all)
        firsts = [gates(heads + e, e, keep_other) for e in range(early)]
        early_copies[2].wait_recv()
        gf[:, extra] = jnp.dot(perm, g_in[...].astype(bf16), preferred_element_type=f32)
        for e in range(early):
            ends[heads + e], _ = chunks(heads + e, *firsts[e])

    for copy in summaries:
        copy.wait_recv()

    def entering(place):
        state_in = jnp.zeros((half, 128), f32)
        adj_in = jnp.zeros((half, 128), f32)
        for s in range(count):
            longer = sums[s, :half] * state_in + sums[s, half : 2 * half]
            state_in = jnp.where(s < place, longer, state_in)
            t = count - 1 - s
            longer = sums[t, :half] * adj_in + sums[t, 2 * half :]
            adj_in = jnp.where(t > place, longer, adj_in)
        return state_in, adj_in

    def lanes_of(value, h):
        return jnp.concatenate([value[h * per + l : h * per + l + 1] for l in range(per)], axis=1)

    def second(u, h, enter):
        ch = slice(u * hd, (u + 1) * hd)
        ex_p, ex_s, ex_q, ex_u = ends[u]
        start = ex_s + ex_p * lanes_of(enter[0], h)
        prev = start
        later = ex_u + ex_q * lanes_of(enter[1], h)
        for i in range(0, steps, 2):
            got = []
            for j in (i, i + 1):
                rs = slice(j * SUB, (j + 1) * SUB)
                state = s_s[rs, ch] + p_s[rs, ch] * start
                adj = la_s[rs, ch] + q_s[rs, ch] * later
                dgate = adj * (c1a_s[rs, ch] * prev + c1b_s[rs, ch])
                own = (state, adj * c3_s[rs, ch]) if u < heads else ()
                got.append((dgate, adj * c2_s[rs, ch]) + own)
                prev = state
            both = slice(i * SUB, (i + 2) * SUB)
            pair = [jnp.concatenate(two) for two in zip(*got)]
            dpre[both, u * hm : u * hm + hd] = pair[0].astype(bf16)
            dpre[both, u * hm + hd : (u + 1) * hm] = pair[1].astype(bf16)
            if u < heads:
                outp[both, ch] = pair[2].astype(bf16)
                gxp[both, ch] = pair[3]

    block = ctxs * (hd // count)

    def product(u, to_dp):
        left = xt[pl.ds(pl.multiple_of(u * hd + to_dp * block, block), block), :]
        return jnp.dot(left, dpre[:, u * hm : (u + 1) * hm], preferred_element_type=f32)

    def shard(flips):
        place = 0
        for i, f in enumerate(flips):
            bit = (my_ctx // (1 << i)) % 2
            place = place + (1 << i) * (1 - bit if f else bit)
        return place

    order = orders(bits)
    stage_one = {}
    stage_two = {}

    def first_stage(h):
        for d in range(1, dps):
            to_dp = lax.rem(my_dp + d, dps)
            gwp[h, to_dp] = product(h, to_dp).reshape(ctxs, hd // count, hm)
            for flips in order:
                k = number(flips)
                stage_one[h, d, k] = send(
                    gwp.at[h, to_dp, shard(flips)], recv1.at[h, d - 1, k],
                    one_send.at[h, d - 1, k], one_recv.at[h, d - 1, k], {"dp": to_dp},
                )

    def mine(h):
        part = product(h, my_dp)
        if h < early:
            part = part + product(heads + h, my_dp)
        gwp[h, my_dp] = part.reshape(ctxs, hd // count, hm)

    def slot(step, flips):
        return sum(1 << (bits - 1 - i) for i in range(step)) + number(flips[step + 1 :])

    def second_stage(h, flips):
        step = flips.index(1) if 1 in flips else bits
        total = gwp[h, my_dp, shard(flips)]
        if h >= early:
            for d in range(1, dps):
                stage_one[h, d, number(flips)].wait_recv()
                total = total + recv1[h, d - 1, number(flips)]
        for i in range(step):
            stage_two[h, slot(i, flips)].wait_recv()
            total = total + recv2[h, slot(i, flips)]
        if step == bits:
            gw_ref[:, h, :] = total
            return
        k = slot(step, flips)
        sbuf[h, k] = total
        bit = (my_ctx // (1 << step)) % 2
        stage_two[h, k] = send(
            sbuf.at[h, k], recv2.at[h, k], two_send.at[h, k], two_recv.at[h, k],
            {"ctx": my_ctx + (1 << step) * (1 - 2 * bit)},
        )

    def finish(h):
        ch = slice(h * hd, (h + 1) * hd)
        back = lax.dot_general(
            dpre[:, h * hm : (h + 1) * hm], w_ref[h], (((1,), (1,)), ((), ())),
            preferred_element_type=f32,
        )
        whole = (gxp[:, ch] + back).astype(bf16)
        gx_ref[:, ch] = jnp.dot(unperm, whole, preferred_element_type=f32).astype(bf16)
        out_ref[:, ch] = jnp.dot(unperm, outp[:, ch], preferred_element_type=f32).astype(bf16)

    enter = entering(me)
    for h in range(early, heads):
        second(h, h, enter)
        first_stage(h)
    for h in range(early):
        second(h, h, enter)
    stores = [
        pltpu.make_async_copy(source, target, stored.at[k])
        for k, (source, target) in enumerate(
            ((out_ref, out_hbm), (gx_ref, gx_hbm), (gw_ref, gw_hbm))
        )
    ]
    enter_other = entering((1 - my_dp) * ctxs + my_ctx) if early else None
    for e in range(early):
        second(heads + e, e, enter_other)
        mine(e)
        for flips in order[: ctxs // 2]:
            second_stage(e, flips)
    for h in range(early, heads):
        mine(h)
    finish(0)
    for h in range(early, heads):
        for flips in order[: ctxs // 2]:
            second_stage(h, flips)
    for h in range(early):
        for flips in order[ctxs // 2 : -1]:
            second_stage(h, flips)
    for h in range(1, heads):
        finish(h)
    stores[0].start()
    stores[1].start()
    for h in range(early, heads):
        for flips in order[ctxs // 2 : -1]:
            second_stage(h, flips)
    for h in range(heads):
        second_stage(h, order[-1])
    stores[2].start()
    for store in stores:
        store.wait()
    for copy in sends:
        copy.wait_send()


def write_out(out_in, gx_in, gw_in, out_hbm, gx_hbm, gw_hbm, out_ref, gx_ref, gw_ref, came, done):
    ins = [
        pltpu.make_async_copy(source, target, came.at[k])
        for k, (source, target) in enumerate(((out_in, out_ref), (gx_in, gx_ref), (gw_in, gw_ref)))
    ]
    outs = [
        pltpu.make_async_copy(source, target, done.at[k])
        for k, (source, target) in enumerate(
            ((out_ref, out_hbm), (gx_ref, gx_hbm), (gw_ref, gw_hbm))
        )
    ]
    for copy in ins:
        copy.start()
    for copy, after in zip(ins, outs):
        copy.wait()
        after.start()
    for copy in outs:
        copy.wait()


def per_device(dps, ctxs, inputs, doc_start, gate_weight, gate_bias, decay_rate, cotangent):
    batch_rows, rows, width = inputs.shape
    hd, heads, hm = gate_weight.shape
    count = dps * ctxs
    early = 0
    lent = max(early, 1) * hd
    f32, bf16 = jnp.float32, jnp.bfloat16
    part = hd // count
    full = pltpu.VMEM((rows, width + lent), f32)
    half = pltpu.VMEM((rows, width), bf16)
    sent = pltpu.VMEM((rows, lent), f32)
    lane_rows = 3 * (width // 128)
    hbm = pl.BlockSpec(memory_space=pltpu.HBM)
    params = dict(vmem_limit_bytes=60 * 1024 * 1024)
    shapes = (
        jax.ShapeDtypeStruct((rows, width), bf16),
        jax.ShapeDtypeStruct((rows, width), bf16),
        jax.ShapeDtypeStruct((part, heads, hm), f32),
    )
    held = pl.pallas_call(
        functools.partial(kernel, dps, ctxs, early),
        out_shape=shapes,
        in_specs=[hbm] * 6,
        out_specs=(hbm,) * 3,
        scratch_shapes=[
            half, pltpu.VMEM((1, rows), jnp.int32), pltpu.VMEM((hd, heads, hm), bf16),
            pltpu.VMEM((heads, hm), f32), pltpu.VMEM((1, width), f32), half,
            pltpu.VMEM((heads, hd, hm), bf16), pltpu.SemaphoreType.DMA((6,)),
            pltpu.VMEM((heads, part, hm), f32), half, half, pltpu.VMEM((part, heads, hm), f32),
            pltpu.SemaphoreType.DMA((3,)),
            sent, sent, pltpu.VMEM((SUB, rows), f32), sent, sent, pltpu.VMEM((SUB, rows), f32),
            full, pltpu.VMEM((rows, width + lent), bf16), pltpu.VMEM((width + lent, rows), bf16),
            full, pltpu.VMEM((rows, (heads + max(early, 1)) * hm), f32),
            full, full, full, full, full, full, full, full, full,
            half, pltpu.VMEM((rows, (heads + max(early, 1)) * hm), bf16),
            pltpu.VMEM((rows, width), f32),
            pltpu.VMEM((count, lane_rows, 128), f32),
            pltpu.VMEM((heads, dps, ctxs, part, hm), f32),
            pltpu.VMEM((heads, dps - 1, ctxs, part, hm), f32),
            pltpu.VMEM((heads, ctxs - 1, part, hm), f32),
            pltpu.VMEM((heads, ctxs - 1, part, hm), f32),
            pltpu.SemaphoreType.DMA((3,)),
            pltpu.SemaphoreType.DMA((3,)),
            pltpu.SemaphoreType.DMA((count - 1,)),
            pltpu.SemaphoreType.DMA((count - 1,)),
            pltpu.SemaphoreType.DMA((heads, dps - 1, ctxs)),
            pltpu.SemaphoreType.DMA((heads, dps - 1, ctxs)),
            pltpu.SemaphoreType.DMA((heads, ctxs - 1)),
            pltpu.SemaphoreType.DMA((heads, ctxs - 1)),
        ],
        compiler_params=pltpu.CompilerParams(collective_id=0, has_side_effects=True, **params),
    )(
        inputs.reshape(rows, width), doc_start.reshape(1, rows), gate_weight, gate_bias,
        decay_rate.reshape(1, width), cotangent.reshape(rows, width),
    )
    out, gx, gw = pl.pallas_call(
        write_out,
        out_shape=shapes,
        in_specs=[hbm] * 3,
        out_specs=(hbm,) * 3,
        scratch_shapes=[
            half, half, pltpu.VMEM((part, heads, hm), f32),
            pltpu.SemaphoreType.DMA((3,)), pltpu.SemaphoreType.DMA((3,)),
        ],
        compiler_params=pltpu.CompilerParams(**params),
    )(*held)
    return (out.reshape(batch_rows, rows, width), gx.reshape(batch_rows, rows, width), gw)


def solution(mesh):
    in_specs = (
        P(None, ("dp", "ctx"), "mp"),
        P(None, ("dp", "ctx")),
        P(None, "mp", None),
        P("mp", None),
        P("mp"),
        P(None, ("dp", "ctx"), "mp"),
    )
    out_specs = (
        P(None, ("dp", "ctx"), "mp"),
        P(None, ("dp", "ctx"), "mp"),
        P(("dp", "ctx"), "mp", None),
    )
    return jax.shard_map(
        functools.partial(per_device, mesh.shape["dp"], mesh.shape["ctx"]),
        mesh=mesh, in_specs=in_specs, out_specs=out_specs, check_vma=False,
    )
```
